32 devices in a mesh: group: 2 (over x), space: 16 (over z, y, core).
Axes of the slice: x: 2, y: 2, z: 4, core: 2. Of those that a mesh axis runs over, the one named last changes fastest.
Arguments:
- node_feat: bfloat16 [8192, 512], P(('group', 'space')), parts along dimension 0, may hold values from -6 to 6
- edge_feat: bfloat16 [32768, 512], P(('group', 'space')), parts along dimension 0, may hold values from -6 to 6
- grad_nodes: bfloat16 [8192, 512], P(('group', 'space')), parts along dimension 0, may hold values from -6 to 6
- grad_edges: bfloat16 [32768, 512], P(('group', 'space')), parts along dimension 0, may hold values from -6 to 6
- edge_first: bfloat16 [1536, 512], replicated, may hold values from -0.15625 to 0.15625
- edge_second: bfloat16 [512, 512], replicated, may hold values from -0.25 to 0.25
- node_first: bfloat16 [1024, 512], replicated, may hold values from -0.1875 to 0.1875
- node_second: bfloat16 [512, 512], replicated, may hold values from -0.25 to 0.25
- gains: float32 [2, 512], replicated, may hold values from 0.1 to 1.9
- edge_peer: int32 [32768], P(('group', 'space')), parts along dimension 0, may hold values from 0 to 15, as said below
- edge_slot: int32 [32768], P(('group', 'space')), parts along dimension 0, may hold values from 0 to 255, as said below
- edge_recv: int32 [32768], P(('group', 'space')), parts along dimension 0, may hold values from 0 to 255
- send_index: int32 [32, 16, 8], P(('group', 'space')), parts along dimension 0, may hold values from 0 to 255
- live_blocks: int32 [32], P(('group', 'space')), parts along dimension 0, may hold values from 1 to 8, as said below
Outputs:
- grad_node_feat: bfloat16 [8192, 512], P(('group', 'space')), parts along dimension 0
- grad_edge_feat: bfloat16 [32768, 512], P(('group', 'space')), parts along dimension 0
- grad_edge_first: float32 [3072, 512], P(('group', 'space')), parts along dimension 0
- grad_edge_second: float32 [1024, 512], P(('group', 'space')), parts along dimension 0
- grad_node_first: float32 [2048, 512], P(('group', 'space')), parts along dimension 0
- grad_node_second: float32 [1024, 512], P(('group', 'space')), parts along dimension 0
- grad_gains: float32 [4, 512], P('group'), parts along dimension 0
The draws below stay inside these ranges and needn't reach their ends.
There are 2 independent parts, one for each index of `group`. The reference program is written for one: setup_inputs(seed, part) draws one part's arguments, and reference() takes and returns one part's arrays. A program takes and returns all parts, laid end to end along the dimension named above; an argument that names none is the same for every part. Nothing has to cross between parts.
Inputs may be any that keep to these rules, and one draw needn't show every extreme that they name: `edge_peer`: the rows of device d name d itself or another device. `edge_slot`: where edge_peer names the edge's own device the value is a local row; else it is a slot below 8. `live_blocks`: some device has all 8 blocks live.
All inputs are finite; a program needn't handle non-finite values.
Results may differ from the reference program's by a relative error of at most 0.008.
Values may be sent and summed in bfloat16 or wider, within the bound.
No kernel may reach another device: no remote copies, remote signals or barrier semaphores. Data moves between devices by JAX's collectives and lax.ppermute only.
A program may use at most 128 MiB of HBM per device.

```python
import jax
import jax.numpy as jnp
from jax import lax

D = 512
NODE_DEV = 256
EDGE_BLOCK = 128
BLOCKS_DEV = 8
CAP = 8
EDGE_DEV = 1024
NODES = 4096
EDGES = 16384
N_SPACE = 16


def edge_choice(key):
    row_device = jnp.arange(EDGES, dtype=jnp.int32) // EDGE_DEV
    remote = jax.random.randint(jax.random.fold_in(key, 101), (EDGES,), 0, 2)
    offset = jax.random.randint(jax.random.fold_in(key, 102), (EDGES,), 1, N_SPACE)
    peer_dev = jnp.where(remote == 1, (row_device + offset) % N_SPACE, row_device)
    return (remote, peer_dev.astype(jnp.int32))


def draw_edge_peer(key, part):
    remote, peer_dev = edge_choice(key)
    return peer_dev


def draw_edge_slot(key, part):
    remote, peer_dev = edge_choice(key)
    key = jax.random.fold_in(key, 2)
    near_node = jax.random.randint(jax.random.fold_in(key, 1), (EDGES,), 0, NODE_DEV)
    far_slot = jax.random.randint(jax.random.fold_in(key, 2), (EDGES,), 0, CAP)
    return jnp.where(remote == 1, far_slot, near_node).astype(jnp.int32)


def draw_live_blocks(key, part):
    key = jax.random.fold_in(key, 3)
    device_ids = jnp.arange(N_SPACE, dtype=jnp.int32)
    base_count = 1 + (BLOCKS_DEV - 1) * device_ids * device_ids // max((N_SPACE - 1) ** 2, 1)
    jitter = jax.random.randint(key, (N_SPACE,), -1, 2)
    block_count = jnp.clip(base_count + jitter, 1, BLOCKS_DEV)
    return jnp.where(device_ids == N_SPACE - 1, BLOCKS_DEV, block_count).astype(jnp.int32)


def with_ends(drawn, rng, smallest, largest):
    index_at = [jax.random.randint(jax.random.fold_in(rng, axis), (), 0, length) for axis, length in enumerate(drawn.shape)]
    main_axis = drawn.shape.index(max(drawn.shape))
    next_to = index_at[:main_axis] + [(index_at[main_axis] + 1) % drawn.shape[main_axis]] + index_at[main_axis + 1:]
    return drawn.at[tuple(index_at)].set(smallest).at[tuple(next_to)].set(largest)


def steps_of(stream_key, shape, shards, low, largest):
    loudness = 1.0
    for dim, shards_of in shards:
        steps = jax.random.uniform(jax.random.fold_in(jax.random.fold_in(stream_key, 6), dim), (shards_of,), jnp.float32, low / len(shards), largest / len(shards))
        loudness = loudness * jnp.repeat(jnp.exp(steps), shape[dim] // shards_of).reshape((-1,) + (1,) * (len(shape) - 1 - dim))
    return loudness


def bell_draw(key, dims, width, most, split=(), held_as=jnp.bfloat16):
    entries = width * jax.random.normal(key, dims, jnp.float32)
    if split:
        entries = entries * steps_of(key, dims, split, -0.22, 0.18)
    return jnp.clip(entries, -most, most).astype(held_as)


def setup_inputs(seed: int = 0, part: int = 0) -> dict:
    key_list = jax.random.split(jax.random.key(seed), 15)
    own_keys = jax.random.split(jax.random.fold_in(key_list[14], part), 15)
    node_feat = bell_draw(own_keys[0], (NODES, D), 1.0, 6.0, ((0, 16),))
    edge_feat = bell_draw(own_keys[1], (EDGES, D), 1.0, 6.0, ((0, 16),))
    grad_nodes = bell_draw(own_keys[2], (NODES, D), 1.0, 6.0, ((0, 16),))
    grad_edges = bell_draw(own_keys[3], (EDGES, D), 1.0, 6.0, ((0, 16),))
    edge_first = bell_draw(key_list[4], (3 * D, D), (3 * D) ** -0.5, 0.15625)
    edge_second = bell_draw(key_list[5], (D, D), D ** -0.5, 0.25)
    node_first = bell_draw(key_list[6], (2 * D, D), (2 * D) ** -0.5, 0.1875)
    node_second = bell_draw(key_list[7], (D, D), D ** -0.5, 0.25)
    gains = jnp.clip(1.0 + 0.18 * jax.random.normal(key_list[8], (2, D), jnp.float32), 0.1, 1.9)
    edge_peer = draw_edge_peer(jax.random.fold_in(jax.random.fold_in(key_list[14], part), 71), part)
    edge_slot = draw_edge_slot(jax.random.fold_in(jax.random.fold_in(key_list[14], part), 71), part)
    edge_recv = with_ends(jax.random.randint(own_keys[11], (EDGES,), 0, NODE_DEV), jax.random.fold_in(own_keys[11], 1), 0, NODE_DEV - 1).astype(jnp.int32)
    send_index = with_ends(jax.random.randint(own_keys[12], (N_SPACE, N_SPACE, CAP), 0, NODE_DEV), jax.random.fold_in(own_keys[12], 1), 0, NODE_DEV - 1).astype(jnp.int32)
    live_blocks = draw_live_blocks(jax.random.fold_in(jax.random.fold_in(key_list[14], part), 71), part)
    return dict(node_feat=node_feat, edge_feat=edge_feat, grad_nodes=grad_nodes, grad_edges=grad_edges, edge_first=edge_first, edge_second=edge_second, node_first=node_first, node_second=node_second, gains=gains, edge_peer=edge_peer, edge_slot=edge_slot, edge_recv=edge_recv, send_index=send_index, live_blocks=live_blocks)


EPS = 1e-05

def times_transposed(left, right):
    return lax.dot_general(left, right, (((1,), (1,)), ((), ())), preferred_element_type=jnp.float32)

def transposed_times(left, right):
    return lax.dot_general(left, right, (((0,), (0,)), ((), ())), preferred_element_type=jnp.float32)

def silu_slope(pre_act):
    sigmoid_val = jax.nn.sigmoid(pre_act)
    return sigmoid_val * (1.0 + pre_act * (1.0 - sigmoid_val))

def mlp_forward(inputs, first_weight, second, gain_row):
    pre_act = jnp.dot(inputs, first_weight, preferred_element_type=jnp.float32)
    hidden = jax.nn.silu(pre_act).astype(jnp.bfloat16)
    post_act = jnp.dot(hidden, second, preferred_element_type=jnp.float32)
    centred = post_act - lax.optimization_barrier(jnp.mean(post_act, axis=-1, keepdims=True))
    inv_std = lax.rsqrt(lax.optimization_barrier(jnp.mean(centred * centred, axis=-1, keepdims=True)) + EPS)
    normed = centred * inv_std
    return (pre_act, hidden, normed, inv_std, normed * gain_row)

def mlp_backward(grad_out, inputs, first_weight, second, gain_row, saved):
    pre_act, hidden, normed, inv_std = saved
    grad_gain = lax.optimization_barrier(jnp.sum(grad_out * normed, axis=0))
    grad_normed = grad_out * gain_row
    grad_post = inv_std * (grad_normed - lax.optimization_barrier(jnp.mean(grad_normed, axis=-1, keepdims=True)) - normed * lax.optimization_barrier(jnp.mean(grad_normed * normed, axis=-1, keepdims=True)))
    grad_post = grad_post.astype(jnp.bfloat16)
    grad_hidden = times_transposed(grad_post, second)
    grad_pre = (grad_hidden * silu_slope(pre_act)).astype(jnp.bfloat16)
    grad_in = times_transposed(grad_pre, first_weight)
    return (grad_in, transposed_times(inputs, grad_pre), transposed_times(hidden, grad_post), grad_gain)

def reference(node_feat, edge_feat, grad_nodes, grad_edges, edge_first, edge_second, node_first, node_second, gains, edge_peer, edge_slot, edge_recv, send_index, live_blocks):
    device_ids = jnp.arange(N_SPACE, dtype=jnp.int32)[:, None]
    peer_dev = edge_peer.reshape(N_SPACE, EDGE_DEV)
    slot_index = edge_slot.reshape(N_SPACE, EDGE_DEV)
    own_dev = jnp.broadcast_to(device_ids, peer_dev.shape)
    far_node = send_index[peer_dev, own_dev, jnp.minimum(slot_index, CAP - 1)]
    senders = jnp.where(peer_dev == own_dev, own_dev * NODE_DEV + slot_index, peer_dev * NODE_DEV + far_node).astype(jnp.int32)
    receivers = (own_dev * NODE_DEV + edge_recv.reshape(N_SPACE, EDGE_DEV)).astype(jnp.int32)
    live_rows = jnp.arange(EDGE_DEV, dtype=jnp.int32)[None, :] < live_blocks[:, None] * EDGE_BLOCK
    edges_dev = edge_feat.reshape(N_SPACE, EDGE_DEV, D)
    grads_dev = grad_edges.reshape(N_SPACE, EDGE_DEV, D)

    def edge_inputs(sender_ids, receiver_ids, features):
        return jnp.concatenate([node_feat[sender_ids], node_feat[receiver_ids], features], axis=1)

    def forward_device(aggregate, pieces):
        sender_ids, receiver_ids, features, live_now = pieces
        outputs = mlp_forward(edge_inputs(sender_ids, receiver_ids, features), edge_first, edge_second, gains[0])
        messages = jnp.where(live_now[:, None], outputs[4], 0.0)
        return (aggregate.at[receiver_ids].add(messages), None)
    aggregate, unused = lax.scan(forward_device, jnp.zeros((NODES, D), jnp.float32), (senders, receivers, edges_dev, live_rows))
    node_inputs = jnp.concatenate([node_feat, aggregate.astype(jnp.bfloat16)], axis=1)
    node_fwd = mlp_forward(node_inputs, node_first, node_second, gains[1])
    node_grad_in, grad_node_first, grad_node_second, node_gain = mlp_backward(grad_nodes.astype(jnp.float32), node_inputs, node_first, node_second, gains[1], node_fwd[:4])
    grad_aggregate = node_grad_in[:, D:].astype(jnp.bfloat16)

    def backward_device(running, pieces):
        totals, first_sum, second_sum, gain_sum = running
        sender_ids, receiver_ids, features, incoming, live_now = pieces
        inputs = edge_inputs(sender_ids, receiver_ids, features)
        outputs = mlp_forward(inputs, edge_first, edge_second, gains[0])
        grad_msg = jnp.where(live_now[:, None], incoming.astype(jnp.float32) + grad_aggregate[receiver_ids].astype(jnp.float32), 0.0)
        grad_in, first_part, second_part, gain_part = mlp_backward(grad_msg, inputs, edge_first, edge_second, gains[0], outputs[:4])
        totals = totals.at[sender_ids].add(grad_in[:, :D]).at[receiver_ids].add(grad_in[:, D:2 * D])
        edge_rows_out = (incoming.astype(jnp.float32) + grad_in[:, 2 * D:]).astype(jnp.bfloat16)
        return ((totals, first_sum + first_part, second_sum + second_part, gain_sum + gain_part), edge_rows_out)
    start_state = (jnp.zeros((NODES, D), jnp.float32), jnp.zeros((3 * D, D), jnp.float32), jnp.zeros((D, D), jnp.float32), jnp.zeros((D,), jnp.float32))
    final_state, edge_rows_out = lax.scan(backward_device, start_state, (senders, receivers, edges_dev, grads_dev, live_rows))
    totals, grad_edge_first, grad_edge_second, edge_gain = final_state
    grad_node_feat = (grad_nodes.astype(jnp.float32) + node_grad_in[:, :D] + totals).astype(jnp.bfloat16)
    return (grad_node_feat, edge_rows_out.reshape(EDGES, D), grad_edge_first, grad_edge_second, grad_node_first, grad_node_second, jnp.stack([edge_gain, node_gain]))
```

```python
import functools

import jax
import jax.numpy as jnp
from jax import lax
from jax.experimental import pallas as pl
from jax.experimental.pallas import tpu as pltpu
from jax.sharding import PartitionSpec as P

EDGE_BLOCK = 128
CHUNK = 256
EPS = 1e-05
BF16 = jnp.bfloat16
F32 = jnp.float32
INT = jnp.int32
MIB = 1 << 20


def dot(left, right):
    return lax.dot_general(left, right, (((1,), (0,)), ((), ())), preferred_element_type=F32)


def times_transposed(left, right):
    return lax.dot_general(left, right, (((1,), (1,)), ((), ())), preferred_element_type=F32)


def transposed_times(left, right):
    return lax.dot_general(left, right, (((0,), (0,)), ((), ())), preferred_element_type=F32)


def ones_where(mask):
    return jnp.where(mask, 1.0, 0.0).astype(BF16)


def columns(row):
    return jnp.transpose(jnp.broadcast_to(row, (EDGE_BLOCK, EDGE_BLOCK)))


def chosen(rows, width):
    lane = lax.broadcasted_iota(INT, (EDGE_BLOCK, EDGE_BLOCK), 1)
    out = []
    for row in rows:
        col = columns(row)
        out.append(
            jnp.concatenate(
                [ones_where(col == lane + EDGE_BLOCK * j) for j in range(width // EDGE_BLOCK)], axis=1
            )
        )
    return jnp.concatenate(out, axis=0)


def chosen_transposed(rows, width):
    sub = lax.broadcasted_iota(INT, (width, EDGE_BLOCK), 0)
    return jnp.concatenate([ones_where(sub == row) for row in rows], axis=1)


def send_choice(table_ref, node_rows):
    devices, capacity = table_ref.shape[1:]
    eye = lax.broadcasted_iota(INT, (capacity, capacity), 0) == lax.broadcasted_iota(
        INT, (capacity, capacity), 1
    )
    lane = lax.broadcasted_iota(INT, (capacity, node_rows), 1).astype(F32)
    out = []
    for j in range(devices):
        row = table_ref[0, j : j + 1, :].astype(F32)
        col = jnp.sum(
            jnp.where(eye, jnp.broadcast_to(row, (capacity, capacity)), 0.0), axis=1, keepdims=True
        )
        out.append(jnp.where(col == lane, 1.0, 0.0))
    return jnp.concatenate(out, axis=0).astype(BF16)


def block_rows(ref, step, count):
    return [ref[pl.ds(step * count + k, 1), :] for k in range(count)]


def live_rows(rows, step, live):
    return [jnp.where(step * len(rows) + k < live, row, -1) for k, row in enumerate(rows)]


def activation(pre):
    sigmoid = 0.5 * jnp.tanh(0.5 * pre) + 0.5
    hidden = pre * sigmoid
    return hidden.astype(BF16), sigmoid + hidden * (1.0 - sigmoid)


def normalize(post):
    centred = post - jnp.mean(post, axis=-1, keepdims=True)
    inv_std = lax.rsqrt(jnp.mean(centred * centred, axis=-1, keepdims=True) + EPS)
    return centred * inv_std, inv_std


def grad_normalize(grad_out, gain, normed, inv_std):
    grad_normed = grad_out * gain
    return (
        inv_std
        * (
            grad_normed
            - jnp.mean(grad_normed, axis=-1, keepdims=True)
            - normed * jnp.mean(grad_normed * normed, axis=-1, keepdims=True)
        )
    ).astype(BF16)


def pack(keep_ref, send_ref, sources, core):
    chips = keep_ref.shape[0]
    for k in range(chips):
        for ref, place in ((keep_ref, 2 * k + core), (send_ref, 2 * k + 1 - core)):
            pieces = []
            for source in sources:
                share = source.shape[0] // (2 * chips)
                pieces.append(source[pl.ds(pl.multiple_of(place * share, 8), share), :])
            ref[k] = jnp.concatenate(pieces, axis=0).astype(BF16)


def outgoing_kernel(node_ref, table_ref, out_ref):
    out_ref[...] = dot(send_choice(table_ref, node_ref.shape[0]), node_ref[...]).astype(BF16)


def prepare_kernel(
    node_ref, edge_ref, first_ref, node_first_ref, peer_ref, slot_ref, recv_ref, part_ref, node_part_ref, table
):
    step = pl.program_id(0)
    own = lax.axis_index("space")
    nodes, width = node_ref.shape

    @pl.when(step == 0)
    def _():
        node = node_ref[...]
        table[0:nodes] = dot(node, first_ref[0:width]).astype(BF16)
        table[nodes:] = dot(node, first_ref[width : 2 * width]).astype(BF16)
        node_part_ref[...] = dot(node, node_first_ref[...])

    count = CHUNK // EDGE_BLOCK
    peers, slots = block_rows(peer_ref, step, count), block_rows(slot_ref, step, count)
    senders = [jnp.where(peer == own, slot, -1) for peer, slot in zip(peers, slots)]
    choice = jnp.concatenate(
        [chosen(senders, nodes), chosen(block_rows(recv_ref, step, count), nodes)], axis=1
    )
    part_ref[...] = dot(edge_ref[...], first_ref[2 * width :]) + dot(choice, table[...])


def forward_kernel(
    part_ref,
    halo_ref,
    first_ref,
    second_ref,
    gains_ref,
    peer_ref,
    slot_ref,
    recv_ref,
    live_ref,
    node_ref,
    node_part_ref,
    node_first_ref,
    node_second_ref,
    grad_nodes_ref,
    slope_ref,
    hidden_ref,
    normed_ref,
    inv_ref,
    grad_agg_ref,
    node_base_ref,
    keep_ref,
    send_ref,
    gain_ref,
    halo_part,
    total,
    grad_first,
    grad_second,
):
    step = pl.program_id(0)
    own = lax.axis_index("space")
    nodes, width = node_ref.shape
    halo_rows = halo_ref.shape[0]
    capacity = halo_rows // (2 * keep_ref.shape[0])

    @pl.when(step == 0)
    def _():
        halo_part[...] = dot(halo_ref[...], first_ref[...]).astype(BF16)
        total[...] = jnp.zeros_like(total)

    count = CHUNK // EDGE_BLOCK
    peers, slots = block_rows(peer_ref, step, count), block_rows(slot_ref, step, count)
    far = [jnp.where(peer == own, -1, peer * capacity + slot) for peer, slot in zip(peers, slots)]
    pre = part_ref[...] + dot(chosen(far, halo_rows), halo_part[...])
    hidden, slope = activation(pre)
    hidden_ref[...] = hidden
    slope_ref[...] = slope.astype(BF16)
    normed, inv_std = normalize(dot(hidden, second_ref[...]))
    normed_ref[...] = normed.astype(BF16)
    inv_ref[...] = jnp.broadcast_to(inv_std, inv_ref.shape)
    messages = (normed * gains_ref[0:1]).astype(BF16)
    receivers = live_rows(block_rows(recv_ref, step, count), step, live_ref[0])
    total[...] += dot(chosen_transposed(receivers, nodes), messages)

    @pl.when(step == pl.num_programs(0) - 1)
    def _():
        aggregate = total[...].astype(BF16)
        node_pre = node_part_ref[...] + dot(aggregate, node_first_ref[width:])
        node_hidden, node_slope = activation(node_pre)
        node_normed, node_inv = normalize(dot(node_hidden, node_second_ref[...]))
        grad_out = grad_nodes_ref[...].astype(F32)
        gain_ref[...] = jnp.sum(grad_out * node_normed, axis=0, keepdims=True)
        grad_post = grad_normalize(grad_out, gains_ref[1:2], node_normed, node_inv)
        grad_pre = (times_transposed(grad_post, node_second_ref[...]) * node_slope).astype(BF16)
        node_base_ref[...] = grad_out + times_transposed(grad_pre, node_first_ref[0:width])
        grad_agg_ref[...] = times_transposed(grad_pre, node_first_ref[width:]).astype(BF16)
        grad_first[0:width] = transposed_times(node_ref[...], grad_pre)
        grad_first[width:] = transposed_times(aggregate, grad_pre)
        grad_second[...] = transposed_times(node_hidden, grad_post)
        pack(keep_ref, send_ref, (grad_first, grad_second), lax.rem(own, 2))


def backward_kernel(
    grad_edges_ref,
    edge_ref,
    slope_ref,
    hidden_ref,
    normed_ref,
    inv_ref,
    grad_agg_ref,
    node_base_ref,
    node_gain_ref,
    node_ref,
    halo_ref,
    first_ref,
    second_ref,
    gains_ref,
    peer_ref,
    slot_ref,
    recv_ref,
    live_ref,
    edge_out_ref,
    node_total_ref,
    back_ref,
    keep_ref,
    send_ref,
    places,
    grad_first,
    grad_second,
    grad_gain,
):
    step = pl.program_id(0)
    own = lax.axis_index("space")
    nodes, width = node_ref.shape
    halo_rows = halo_ref.shape[0]
    devices = 2 * keep_ref.shape[0]
    capacity = halo_rows // devices

    @pl.when(step == 0)
    def _():
        places[...] = jnp.zeros_like(places)
        grad_first[...] = jnp.zeros_like(grad_first)
        grad_second[...] = jnp.zeros_like(grad_second)
        grad_gain[...] = jnp.zeros_like(grad_gain)

    count = CHUNK // EDGE_BLOCK
    peers, slots = block_rows(peer_ref, step, count), block_rows(slot_ref, step, count)
    receivers = live_rows(block_rows(recv_ref, step, count), step, live_ref[0])
    senders = [
        jnp.where(peer == own, slot, nodes + peer * capacity + slot) for peer, slot in zip(peers, slots)
    ]
    incoming = grad_edges_ref[...].astype(F32)
    live = jnp.concatenate(
        [
            jnp.where(jnp.full((EDGE_BLOCK, 1), step * count + k, INT) < live_ref[0], 1.0, 0.0)
            for k in range(count)
        ],
        axis=0,
    )
    grad_out = incoming * live + dot(chosen(receivers, nodes), grad_agg_ref[...])
    normed = normed_ref[...].astype(F32)
    grad_gain[...] += jnp.sum(grad_out * normed, axis=0, keepdims=True)
    grad_post = grad_normalize(grad_out, gains_ref[0:1], normed, inv_ref[:, 0:1])
    grad_pre = (times_transposed(grad_post, second_ref[...]) * slope_ref[...].astype(F32)).astype(BF16)
    edge_out_ref[...] = (incoming + times_transposed(grad_pre, first_ref[2 * width :])).astype(BF16)
    choice = jnp.concatenate(
        [chosen_transposed(senders, nodes + halo_rows), chosen_transposed(receivers, nodes)], axis=0
    )
    places[...] += dot(choice, grad_pre)
    grad_first[2 * width :] += transposed_times(edge_ref[...], grad_pre)
    grad_second[...] += transposed_times(hidden_ref[...], grad_post)

    @pl.when(step == pl.num_programs(0) - 1)
    def _():
        near = places[0:nodes].astype(BF16)
        far = places[nodes : nodes + halo_rows].astype(BF16)
        received = places[nodes + halo_rows :].astype(BF16)
        node = node_ref[...]
        back = times_transposed(far, first_ref[0:width])
        gains = jnp.concatenate([grad_gain[...], node_gain_ref[...]], axis=0)
        coarse = gains.astype(BF16).astype(F32)
        tail = jnp.concatenate(
            [coarse, gains - coarse, jnp.zeros((4, width), F32)], axis=0
        )
        for k in range(devices):
            back_ref[k] = jnp.concatenate(
                [back[k * capacity : (k + 1) * capacity], tail], axis=0
            ).astype(BF16)
        node_total_ref[...] = (
            node_base_ref[...]
            + times_transposed(near, first_ref[0:width])
            + times_transposed(received, first_ref[width : 2 * width])
        )
        grad_first[0:width] = transposed_times(node, near) + transposed_times(halo_ref[...], far)
        grad_first[width : 2 * width] = transposed_times(node, received)
        pack(keep_ref, send_ref, (grad_first, grad_second), lax.rem(own, 2))


def nodes_kernel(total_ref, returned_ref, table_ref, out_ref, gains_ref):
    devices, capacity = table_ref.shape[1:]
    rows = [returned_ref[k].astype(F32) for k in range(devices)]
    returned = jnp.concatenate([row[0:capacity] for row in rows], axis=0).astype(BF16)
    choice = send_choice(table_ref, total_ref.shape[0])
    out_ref[...] = (total_ref[...] + transposed_times(choice, returned)).astype(BF16)
    tail = rows[0][capacity:]
    for row in rows[1:]:
        tail = tail + row[capacity:]
    gains_ref[...] = tail[0:2] + tail[2:4]


def whole(array):
    zeros = (0,) * array.ndim
    return pl.BlockSpec(array.shape, lambda i: zeros)


def chunked(array):
    return pl.BlockSpec((CHUNK, array.shape[1]), lambda i: (i, 0))


SCALAR = pl.BlockSpec(memory_space=pltpu.SMEM)


def shaped(*shape, dtype=F32):
    return jax.ShapeDtypeStruct(shape, dtype)


def call(body, steps, operands, specs, outs, out_specs, scratch=(), flops=0, name=None):
    moved = sum(a.size * a.dtype.itemsize for a in (*operands, *outs))
    return pl.pallas_call(
        body,
        grid=(steps,),
        in_specs=specs,
        out_specs=out_specs,
        out_shape=outs,
        scratch_shapes=scratch,
        name=name,
        cost_estimate=pl.CostEstimate(flops=flops, bytes_accessed=moved, transcendentals=0),
        compiler_params=pltpu.CompilerParams(vmem_limit_bytes=32 * MIB),
    )(*operands)


def shards(
    node_feat,
    edge_feat,
    grad_nodes,
    grad_edges,
    edge_first,
    edge_second,
    node_first,
    node_second,
    gains,
    edge_peer,
    edge_slot,
    edge_recv,
    send_index,
    live_blocks,
):
    nodes, width = node_feat.shape
    edges = edge_feat.shape[0]
    devices, capacity = send_index.shape[1:]
    chips = devices // 2
    halo_rows = devices * capacity
    steps = edges // CHUNK
    peer, slot, recv = (a.reshape(edges // EDGE_BLOCK, EDGE_BLOCK) for a in (edge_peer, edge_slot, edge_recv))
    other_core = [(i, i ^ 1) for i in range(devices)]
    same_core = [[core + 2 * k for k in range(chips)] for core in range(2)]
    block = width * width * 2

    outgoing = call(
        outgoing_kernel,
        1,
        (node_feat, send_index),
        [whole(node_feat), whole(send_index)],
        [shaped(halo_rows, width, dtype=BF16)],
        [pl.BlockSpec((halo_rows, width), lambda i: (0, 0))],
        name="outgoing",
    )[0].reshape(devices, capacity, width)
    halo = lax.all_to_all(outgoing, "space", split_axis=0, concat_axis=0, tiled=True).reshape(halo_rows, width)

    part, node_part = call(
        prepare_kernel,
        steps,
        (node_feat, edge_feat, edge_first, node_first, peer, slot, recv),
        [
            whole(node_feat),
            chunked(edge_feat),
            whole(edge_first),
            pl.BlockSpec((width, width), lambda i: (0, 0)),
            whole(peer),
            whole(slot),
            whole(recv),
        ],
        [shaped(edges, width), shaped(nodes, width)],
        [pl.BlockSpec((CHUNK, width), lambda i: (i, 0)), pl.BlockSpec((nodes, width), lambda i: (0, 0))],
        [pltpu.VMEM((2 * nodes, width), BF16)],
        flops=block * (2 * edges + 3 * nodes),
        name="prepare",
    )

    node_share = node_first.shape[0] // devices + node_second.shape[0] // devices
    node_packed = shaped(chips, node_share, width, dtype=BF16)
    forward_in = (
        part,
        halo,
        edge_first,
        edge_second,
        gains,
        peer,
        slot,
        recv,
        live_blocks,
        node_feat,
        node_part,
        node_first,
        node_second,
        grad_nodes,
    )
    forward_specs = [whole(a) for a in forward_in]
    forward_specs[0] = chunked(part)
    forward_specs[2] = pl.BlockSpec((width, width), lambda i: (0, 0))
    forward_specs[8] = SCALAR
    rows_out = [
        shaped(edges, width, dtype=BF16),
        shaped(edges, width, dtype=BF16),
        shaped(edges, width, dtype=BF16),
        shaped(edges, 128),
    ]
    forward_out = [
        *rows_out,
        shaped(nodes, width, dtype=BF16),
        shaped(nodes, width),
        node_packed,
        node_packed,
        shaped(1, width),
    ]
    slope, hidden, normed, inv_std, grad_agg, node_base, node_keep, node_send, node_gain = call(
        forward_kernel,
        steps,
        forward_in,
        forward_specs,
        forward_out,
        [*(chunked(a) for a in rows_out), *(whole(a) for a in forward_out[4:])],
        [
            pltpu.VMEM((halo_rows, width), BF16),
            pltpu.VMEM((nodes, width), F32),
            pltpu.VMEM(node_first.shape, F32),
            pltpu.VMEM(node_second.shape, F32),
        ],
        flops=block * (2 * edges + 9 * nodes),
        name="forward",
    )

    def spread(keep, received):
        both = (keep.astype(F32) + received.astype(F32)).astype(BF16)
        return lax.all_to_all(
            both, "space", split_axis=0, concat_axis=0, tiled=True, axis_index_groups=same_core
        )

    node_received = lax.ppermute(node_send, "space", other_core)
    node_spread = spread(node_keep, node_received)

    edge_share = edge_first.shape[0] // devices + edge_second.shape[0] // devices
    edge_packed = shaped(chips, edge_share, width, dtype=BF16)
    backward_in = (
        grad_edges,
        edge_feat,
        slope,
        hidden,
        normed,
        inv_std,
        grad_agg,
        node_base,
        node_gain,
        node_feat,
        halo,
        edge_first,
        edge_second,
        gains,
        peer,
        slot,
        recv,
        live_blocks,
    )
    backward_specs = [*(chunked(a) for a in backward_in[:6]), *(whole(a) for a in backward_in[6:-1]), SCALAR]
    backward_out = [
        shaped(edges, width, dtype=BF16),
        shaped(nodes, width),
        shaped(devices, 2 * capacity, width, dtype=BF16),
        edge_packed,
        edge_packed,
    ]
    grad_edge_feat, node_total, back, edge_keep, edge_send = call(
        backward_kernel,
        steps,
        backward_in,
        backward_specs,
        backward_out,
        [chunked(backward_out[0]), *(whole(a) for a in backward_out[1:])],
        [
            pltpu.VMEM((2 * nodes + halo_rows, width), F32),
            pltpu.VMEM(edge_first.shape, F32),
            pltpu.VMEM(edge_second.shape, F32),
            pltpu.VMEM((1, width), F32),
        ],
        flops=block * (6 * edges),
        name="backward",
    )

    edge_received = lax.ppermute(edge_send, "space", other_core)
    returned = lax.all_to_all(back, "space", split_axis=0, concat_axis=0, tiled=True)
    edge_spread = spread(edge_keep, edge_received)

    node_out = [shaped(nodes, width, dtype=BF16), shaped(2, width)]
    grad_node_feat, gain_totals = call(
        nodes_kernel,
        1,
        (node_total, returned, send_index),
        [whole(node_total), whole(returned), whole(send_index)],
        node_out,
        [whole(a) for a in node_out],
        name="nodes",
    )

    edge_sum = jnp.sum(edge_spread.astype(F32), axis=0)
    node_sum = jnp.sum(node_spread.astype(F32), axis=0)
    edge_cut = edge_first.shape[0] // devices
    node_cut = node_first.shape[0] // devices
    return (
        grad_node_feat,
        grad_edge_feat,
        edge_sum[:edge_cut],
        edge_sum[edge_cut:],
        node_sum[:node_cut],
        node_sum[node_cut:],
        gain_totals,
    )


def solution(mesh):
    placed = (
        P(("group", "space"), None),
        P(("group", "space"), None),
        P(("group", "space"), None),
        P(("group", "space"), None),
        P(),
        P(),
        P(),
        P(),
        P(),
        P(("group", "space")),
        P(("group", "space")),
        P(("group", "space")),
        P(("group", "space"), None, None),
        P(("group", "space")),
    )
    return jax.shard_map(
        shards,
        mesh=mesh,
        in_specs=placed,
        out_specs=(
            P(("group", "space"), None),
            P(("group", "space"), None),
            P(("group", "space"), None),
            P(("group", "space"), None),
            P(("group", "space"), None),
            P(("group", "space"), None),
            P("group", None),
        ),
        check_vma=False,
    )
```

```python
import functools

import jax
import jax.numpy as jnp
from jax import lax
from jax.experimental import pallas as pl
from jax.experimental.pallas import tpu as pltpu
from jax.sharding import PartitionSpec as P

EDGE_BLOCK = 128
CHUNK = 256
EPS = 1e-05
BF16 = jnp.bfloat16
F32 = jnp.float32
INT = jnp.int32
MIB = 1 << 20


def dot(left, right):
    return lax.dot_general(left, right, (((1,), (0,)), ((), ())), preferred_element_type=F32)


def times_transposed(left, right):
    return lax.dot_general(left, right, (((1,), (1,)), ((), ())), preferred_element_type=F32)


def transposed_times(left, right):
    return lax.dot_general(left, right, (((0,), (0,)), ((), ())), preferred_element_type=F32)


def ones_where(mask):
    return jnp.where(mask, 1.0, 0.0).astype(BF16)


def chosen(row, width):
    lane = lax.broadcasted_iota(INT, (EDGE_BLOCK, EDGE_BLOCK), 1)
    col = jnp.transpose(jnp.broadcast_to(row, (EDGE_BLOCK, EDGE_BLOCK)))
    return jnp.concatenate(
        [ones_where(col == lane + EDGE_BLOCK * j) for j in range(width // EDGE_BLOCK)], axis=1
    )


def chosen_transposed(row, width):
    return ones_where(lax.broadcasted_iota(INT, (width, EDGE_BLOCK), 0) == row)


def send_choice(table_ref, node_rows):
    capacity, devices = table_ref.shape[1:]
    lane = lax.broadcasted_iota(INT, (capacity, node_rows), 1)
    table = table_ref[0]
    out = [jnp.where(table[:, j : j + 1] == lane, 1.0, 0.0) for j in range(devices)]
    return jnp.concatenate(out, axis=0).astype(BF16)


def activation(pre):
    sigmoid = 0.5 * jnp.tanh(0.5 * pre) + 0.5
    hidden = pre * sigmoid
    return hidden.astype(BF16), sigmoid + hidden * (1.0 - sigmoid)


def normalize(post):
    centred = post - jnp.mean(post, axis=-1, keepdims=True)
    inv_std = lax.rsqrt(jnp.mean(centred * centred, axis=-1, keepdims=True) + EPS)
    return centred * inv_std, inv_std


def grad_normalize(grad_out, gain, normed, inv_std):
    grad_normed = grad_out * gain
    return (
        inv_std
        * (
            grad_normed
            - jnp.mean(grad_normed, axis=-1, keepdims=True)
            - normed * jnp.mean(grad_normed * normed, axis=-1, keepdims=True)
        )
    ).astype(BF16)


def pack(keep_ref, send_ref, stage, sems, sources, core):
    chips = stage.shape[0]
    copies = []
    for away in (True, False):
        for k in range(chips):
            place = 2 * k + 1 - core if away else 2 * k + core
            pieces = []
            for source in sources:
                share = source.shape[0] // (2 * chips)
                pieces.append(source[pl.ds(pl.multiple_of(place * share, 8), share), :])
            rows = jnp.concatenate(pieces, axis=0).astype(BF16)
            if away:
                stage[k] = rows
                copies.append(pltpu.make_async_copy(stage.at[k], send_ref.at[k], sems.at[k]))
                copies[-1].start()
            else:
                keep_ref[k] = rows
    return copies


def outgoing_kernel(node_hbm, table_hbm, out_ref, node, table, stage, sems):
    copies = [
        pltpu.make_async_copy(node_hbm, node, sems.at[0]),
        pltpu.make_async_copy(table_hbm, table, sems.at[1]),
    ]
    for copy in copies:
        copy.start()
    copies[1].wait()
    choice = send_choice(table, node.shape[0])
    copies[0].wait()
    stage[...] = dot(choice, node[...]).astype(BF16)
    copy = pltpu.make_async_copy(stage, out_ref, sems.at[0])
    copy.start()
    copy.wait()


def load(sources, targets, sems):
    copies = [
        pltpu.make_async_copy(source, target, sems.at[k])
        for k, (source, target) in enumerate(zip(sources, targets))
    ]
    for copy in copies:
        copy.start()
    return copies


def prepare_kernel(
    live_ref,
    peer_hbm,
    slot_hbm,
    recv_hbm,
    node_hbm,
    first_hbm,
    edge_hbm,
    node_first_hbm,
    second_hbm,
    part_ref,
    far_ref,
    top_ref,
    second_ref,
    node_part_ref,
    receive_ref,
    place_ref,
    peer_ref,
    slot_ref,
    recv_ref,
    node,
    first,
    edge,
    node_first,
    node_part,
    receive,
    places,
    table,
    sems,
    out_sems,
):
    nodes, width = node.shape
    copies = load(
        (
            peer_hbm,
            slot_hbm,
            recv_hbm,
            node_hbm,
            first_hbm,
            edge_hbm,
            node_first_hbm.at[pl.ds(0, width)],
            second_hbm,
            first_hbm.at[pl.ds(0, width)],
        ),
        (peer_ref, slot_ref, recv_ref, node, first, edge, node_first, second_ref, top_ref),
        sems,
    )
    own = lax.axis_index("space")
    blocks = peer_ref.shape[0]
    halo_rows = far_ref.shape[1]
    capacity = halo_rows // lax.axis_size("space")
    for k in range(3):
        copies[k].wait()
    near = []
    for b in range(blocks):
        rows = pl.ds(b * EDGE_BLOCK, EDGE_BLOCK)
        peer, slot, recv = (ref[b : b + 1, :] for ref in (peer_ref, slot_ref, recv_ref))
        mine = peer == own
        far = peer * capacity + slot
        near.append(chosen(jnp.where(mine, slot, -1), nodes))
        far_ref[rows, :] = chosen(jnp.where(mine, -1, far), halo_rows)
        received = jnp.where(b < live_ref[0], recv, -1)
        receive[rows, :] = chosen(received, nodes)
        places[0 : nodes + halo_rows, rows] = chosen_transposed(
            jnp.where(mine, slot, nodes + far), nodes + halo_rows
        )
        places[nodes + halo_rows :, rows] = chosen_transposed(received, nodes)
    out_copies = load((receive, places), (receive_ref, place_ref), out_sems)
    copies[3].wait()
    copies[4].wait()
    table[0:nodes] = dot(node[...], first[0:width]).astype(BF16)
    table[nodes:] = dot(node[...], first[width : 2 * width]).astype(BF16)
    copies[5].wait()
    count = CHUNK // EDGE_BLOCK
    for c in range(blocks // count):
        rows = pl.ds(c * CHUNK, CHUNK)
        choice = jnp.concatenate(
            [jnp.concatenate(near[c * count : (c + 1) * count], axis=0), receive[rows, :]], axis=1
        )
        part_ref[rows, :] = dot(edge[rows, :], first[2 * width :]) + dot(choice, table[...])
    copies[6].wait()
    node_part[...] = dot(node[...], node_first[...])
    out_copies.append(pltpu.make_async_copy(node_part, node_part_ref, out_sems.at[2]))
    out_copies[2].start()
    for copy in (*copies[7:], *out_copies):
        copy.wait()


def forward_kernel(
    part_ref,
    halo_ref,
    far_ref,
    top_ref,
    second_ref,
    gains_hbm,
    place_hbm,
    node_part_hbm,
    node_first_hbm,
    node_second_hbm,
    grad_nodes_hbm,
    node_hbm,
    slope_ref,
    hidden_ref,
    normed_ref,
    inv_ref,
    grad_agg_ref,
    node_gain_ref,
    keep_ref,
    node_base_ref,
    send_ref,
    gains,
    place,
    node_part,
    node_first,
    node_second,
    grad_nodes,
    node,
    messages,
    grad_first,
    grad_second,
    node_base,
    stage,
    sems,
    out_sems,
    base_sem,
):
    nodes, width = node.shape
    copies = load(
        (
            gains_hbm,
            place_hbm.at[pl.ds(place_hbm.shape[0] - nodes, nodes)],
            node_part_hbm,
            node_first_hbm,
            node_second_hbm,
            grad_nodes_hbm,
            node_hbm,
        ),
        (gains, place, node_part, node_first, node_second, grad_nodes, node),
        sems,
    )
    halo_part = dot(halo_ref[...], top_ref[...]).astype(BF16)
    copies[0].wait()
    for c in range(part_ref.shape[0] // CHUNK):
        rows = pl.ds(c * CHUNK, CHUNK)
        hidden, slope = activation(part_ref[rows, :] + dot(far_ref[rows, :], halo_part))
        hidden_ref[rows, :] = hidden
        slope_ref[rows, :] = slope.astype(BF16)
        normed, inv_std = normalize(dot(hidden, second_ref[...]))
        normed_ref[rows, :] = normed.astype(BF16)
        inv_ref[rows, :] = jnp.broadcast_to(inv_std, (CHUNK, inv_ref.shape[1]))
        messages[rows, :] = (normed * gains[0:1]).astype(BF16)
    for copy in copies[1:]:
        copy.wait()
    aggregate = dot(place[...], messages[...]).astype(BF16)
    node_hidden, node_slope = activation(node_part[...] + dot(aggregate, node_first[width:]))
    node_normed, node_inv = normalize(dot(node_hidden, node_second[...]))
    grad_out = grad_nodes[...].astype(F32)
    node_gain_ref[...] = jnp.sum(grad_out * node_normed, axis=0, keepdims=True)
    grad_post = grad_normalize(grad_out, gains[1:2], node_normed, node_inv)
    grad_second[...] = transposed_times(node_hidden, grad_post)
    grad_pre = (times_transposed(grad_post, node_second[...]) * node_slope).astype(BF16)
    grad_first[0:width] = transposed_times(node[...], grad_pre)
    grad_first[width:] = transposed_times(aggregate, grad_pre)
    core = lax.rem(lax.axis_index("space"), 2)
    copies = pack(keep_ref, send_ref, stage, out_sems, (grad_first, grad_second), core)
    node_base[...] = grad_out + times_transposed(grad_pre, node_first[0:width])
    copies.append(pltpu.make_async_copy(node_base, node_base_ref, base_sem.at[0]))
    copies[-1].start()
    grad_agg_ref[...] = times_transposed(grad_pre, node_first[width:]).astype(BF16)
    for copy in copies:
        copy.wait()


def backward_kernel(
    live_ref,
    grad_edges_ref,
    slope_ref,
    hidden_ref,
    normed_ref,
    inv_ref,
    grad_agg_ref,
    node_gain_ref,
    halo_ref,
    second_ref,
    receive_ref,
    first_ref,
    gains_ref,
    place_hbm,
    edge_hbm,
    node_hbm,
    node_base_hbm,
    keep_ref,
    node_total_ref,
    edge_out_ref,
    back_ref,
    send_ref,
    place_ref,
    edge_ref,
    node_ref,
    node_base,
    grad_post_all,
    grad_pre_all,
    edge_out,
    back_stage,
    grad_first,
    grad_second,
    stage,
    sems,
    edge_sems,
    back_sems,
    load_sems,
):
    nodes, width = node_ref.shape
    loads = load(
        (place_hbm, edge_hbm, node_hbm, node_base_hbm), (place_ref, edge_ref, node_ref, node_base), load_sems
    )
    halo_rows = halo_ref.shape[0]
    devices = back_ref.shape[0]
    capacity = halo_rows // devices
    count = CHUNK // EDGE_BLOCK
    edge_copies = []
    grad_gain = jnp.zeros((1, width), F32)
    for c in range(edge_ref.shape[0] // CHUNK):
        rows = pl.ds(c * CHUNK, CHUNK)
        incoming = grad_edges_ref[rows, :].astype(F32)
        live = jnp.concatenate(
            [
                jnp.where(jnp.full((EDGE_BLOCK, 1), c * count + k, INT) < live_ref[0], 1.0, 0.0)
                for k in range(count)
            ],
            axis=0,
        )
        grad_out = incoming * live + dot(receive_ref[rows, :], grad_agg_ref[...])
        normed = normed_ref[rows, :].astype(F32)
        grad_gain += jnp.sum(grad_out * normed, axis=0, keepdims=True)
        grad_post = grad_normalize(grad_out, gains_ref[0:1], normed, inv_ref[rows, 0:1])
        grad_post_all[rows, :] = grad_post
        grad_pre = (times_transposed(grad_post, second_ref[...]) * slope_ref[rows, :].astype(F32)).astype(BF16)
        grad_pre_all[rows, :] = grad_pre
        edge_out[rows, :] = (incoming + times_transposed(grad_pre, first_ref[2 * width :])).astype(BF16)
        copy = pltpu.make_async_copy(edge_out.at[rows], edge_out_ref.at[rows], edge_sems.at[c])
        copy.start()
        edge_copies.append(copy)
    for copy in loads:
        copy.wait()
    places = dot(place_ref[...], grad_pre_all[...])
    near = places[0:nodes].astype(BF16)
    far = places[nodes : nodes + halo_rows].astype(BF16)
    received = places[nodes + halo_rows :].astype(BF16)
    back = times_transposed(far, first_ref[0:width])
    gains = jnp.concatenate([grad_gain, node_gain_ref[...]], axis=0)
    coarse = gains.astype(BF16).astype(F32)
    tail = jnp.concatenate(
        [coarse, gains - coarse, jnp.zeros((back_ref.shape[1] - capacity - 4, width), F32)], axis=0
    )
    for k in range(devices):
        back_stage[k] = jnp.concatenate([back[k * capacity : (k + 1) * capacity], tail], axis=0).astype(BF16)
    back_copy = pltpu.make_async_copy(back_stage, back_ref, back_sems.at[0])
    back_copy.start()
    grad_second[...] = transposed_times(hidden_ref[...], grad_post_all[...])
    grad_first[2 * width :] = transposed_times(edge_ref[...], grad_pre_all[...])
    grad_first[0:width] = transposed_times(node_ref[...], near) + transposed_times(halo_ref[...], far)
    grad_first[width : 2 * width] = transposed_times(node_ref[...], received)
    core = lax.rem(lax.axis_index("space"), 2)
    copies = pack(keep_ref, send_ref, stage, sems, (grad_first, grad_second), core)
    node_base[...] += times_transposed(near, first_ref[0:width]) + times_transposed(
        received, first_ref[width : 2 * width]
    )
    total_copy = pltpu.make_async_copy(node_base, node_total_ref, back_sems.at[1])
    total_copy.start()
    for copy in (*edge_copies, back_copy, total_copy, *copies):
        copy.wait()


def nodes_kernel(total_hbm, returned_ref, table_hbm, out_ref, gains_ref, total, table, stage, gain_stage, sems):
    loads = load((total_hbm, table_hbm), (total, table), sems)
    capacity, devices = table.shape[1:]
    rows = [returned_ref[k].astype(F32) for k in range(devices)]
    returned = jnp.concatenate([row[0:capacity] for row in rows], axis=0).astype(BF16)
    tail = rows[0][capacity:]
    for row in rows[1:]:
        tail = tail + row[capacity:]
    gain_stage[...] = tail[0:2] + tail[2:4]
    for copy in loads:
        copy.wait()
    choice = send_choice(table, total.shape[0])
    stage[...] = (total[...] + transposed_times(choice, returned)).astype(BF16)
    for copy in load((stage, gain_stage), (out_ref, gains_ref), sems):
        copy.wait()


def exchange_orders(chips):
    bits = list(range(chips.bit_length() - 1))
    return bits, [*bits[1::-1], *bits[2:]]


def exchange(sent, bits, devices):
    return [
        lax.ppermute(piece, "space", [(i, i ^ (2 << bit)) for i in range(devices)])
        for piece, bit in zip(sent, bits)
    ]


def half_of(step, bit, position, away):
    value = (lax.axis_index("space") >> (bit + 1)) & 1
    value = 1 - value if away else value
    low = step & ((1 << position) - 1)
    return ((step >> position) << (position + 1)) | (value << position) | low


def fold(sums, sent, kept, stages, sems, bits, positions):
    copies = []
    for away in (True, False):
        for half, (bit, position) in enumerate(zip(bits, positions)):
            for k in range(kept[half].shape[0]):
                block = sums(half, half_of(k, bit, position, away)).astype(BF16)
                if away:
                    stages[half][k] = block
                    copies.append(
                        pltpu.make_async_copy(stages[half].at[k], sent[half].at[k], sems[half].at[k])
                    )
                    copies[-1].start()
                else:
                    kept[half][k] = block
    for copy in copies:
        copy.wait()


def first_fold_kernel(bits, node_keep, node_received, edge_keep, edge_received, *refs):
    def sums(half, place):
        columns = pl.ds(half * refs[0].shape[2], refs[0].shape[2])
        return jnp.concatenate(
            [
                kept[place, :, columns].astype(F32) + received[place, :, columns].astype(F32)
                for kept, received in ((node_keep, node_received), (edge_keep, edge_received))
            ],
            axis=0,
        )

    fold(sums, refs[0:2], refs[2:4], refs[4:6], refs[6:8], bits, bits)


def later_fold_kernel(bits, positions, *refs):
    def sums(half, place):
        return refs[half][place].astype(F32) + refs[2 + half][place].astype(F32)

    fold(sums, refs[4:6], refs[6:8], refs[8:10], refs[10:12], bits, positions)


def shares_kernel(left, right, left_in, right_in, *refs):
    outs, stages, sems = refs[:4], refs[4:8], refs[8]
    total = jnp.concatenate(
        [a[0].astype(F32) + b[0].astype(F32) for a, b in ((left, left_in), (right, right_in))], axis=1
    )
    start = 0
    copies = []
    for k, (out, stage) in enumerate(zip(outs, stages)):
        stage[...] = total[start : start + out.shape[0]]
        start += out.shape[0]
        copies.append(pltpu.make_async_copy(stage, out, sems.at[k]))
        copies[-1].start()
    for copy in copies:
        copy.wait()


VMEM, HBM, SMEM = pltpu.VMEM, pltpu.HBM, pltpu.SMEM


def call(body, name, operands, outs, scratch=(), flops=0):
    spaces = [space for _, space in operands]
    arrays = [
        array if space is SMEM else pltpu.with_memory_space_constraint(array, space) for array, space in operands
    ]
    moved = sum(a.size * a.dtype.itemsize for a, _ in operands)
    return pl.pallas_call(
        body,
        in_specs=[pl.BlockSpec(memory_space=space) for space in spaces],
        out_specs=[pl.BlockSpec(memory_space=space) for space, _, _ in outs],
        out_shape=[space(shape, dtype) for space, shape, dtype in outs],
        scratch_shapes=scratch,
        name=name,
        cost_estimate=pl.CostEstimate(flops=flops, bytes_accessed=moved, transcendentals=0),
        compiler_params=pltpu.CompilerParams(vmem_limit_bytes=24 * MIB),
    )(*arrays)


def semaphores(count):
    return pltpu.SemaphoreType.DMA((count,))


def fold_call(body, name, operands, shape):
    out = call(
        body,
        name,
        [(array, VMEM) for array in operands],
        [(HBM, shape, BF16), (HBM, shape, BF16), (VMEM, shape, BF16), (VMEM, shape, BF16)],
        [VMEM(shape, BF16), VMEM(shape, BF16), semaphores(shape[0]), semaphores(shape[0])],
    )
    return out[:2], out[2:]


def shards(
    node_feat,
    edge_feat,
    grad_nodes,
    grad_edges,
    edge_first,
    edge_second,
    node_first,
    node_second,
    gains,
    edge_peer,
    edge_slot,
    edge_recv,
    send_index,
    live_blocks,
):
    nodes, width = node_feat.shape
    edges = edge_feat.shape[0]
    devices, capacity = send_index.shape[1:]
    chips = devices // 2
    halo_rows = devices * capacity
    peer, slot, recv = (a.reshape(edges // EDGE_BLOCK, EDGE_BLOCK) for a in (edge_peer, edge_slot, edge_recv))
    other_core = [(i, i ^ 1) for i in range(devices)]
    block = width * width * 2

    send_table = jnp.swapaxes(send_index, 1, 2)
    (outgoing,) = call(
        outgoing_kernel,
        "outgoing",
        [(node_feat, HBM), (send_table, HBM)],
        [(HBM, (halo_rows, width), BF16)],
        [
            VMEM(node_feat.shape, BF16),
            VMEM(send_table.shape, INT),
            VMEM((halo_rows, width), BF16),
            semaphores(2),
        ],
    )
    halo = lax.all_to_all(
        outgoing.reshape(devices, capacity, width), "space", split_axis=0, concat_axis=0, tiled=True
    ).reshape(halo_rows, width)

    rows_bf16, nodes_f32 = (edges, width), (nodes, width)
    top_shape, place_shape = (width, width), (2 * nodes + halo_rows, edges)
    part, far, top, second, node_part, receive, place = call(
        prepare_kernel,
        "prepare",
        [
            (live_blocks, SMEM),
            *(
                (a, HBM)
                for a in (peer, slot, recv, node_feat, edge_first, edge_feat, node_first, edge_second)
            ),
        ],
        [
            (VMEM, rows_bf16, F32),
            (VMEM, (edges, halo_rows), BF16),
            (VMEM, top_shape, BF16),
            (VMEM, edge_second.shape, BF16),
            (HBM, nodes_f32, F32),
            (HBM, (edges, nodes), BF16),
            (HBM, place_shape, BF16),
        ],
        [
            VMEM(peer.shape, INT),
            VMEM(slot.shape, INT),
            VMEM(recv.shape, INT),
            VMEM(node_feat.shape, BF16),
            VMEM(edge_first.shape, BF16),
            VMEM(edge_feat.shape, BF16),
            VMEM(top_shape, BF16),
            VMEM(nodes_f32, F32),
            VMEM((edges, nodes), BF16),
            VMEM(place_shape, BF16),
            VMEM((2 * nodes, width), BF16),
            semaphores(9),
            semaphores(3),
        ],
        flops=block * (2 * edges + 3 * nodes),
    )

    share = node_first.shape[0] // devices + node_second.shape[0] // devices
    slope, hidden, normed, inv_std, grad_agg, node_gain, node_keep, node_base, node_send = call(
        forward_kernel,
        "forward",
        [
            *((a, VMEM) for a in (part, halo, far, top, second)),
            *((a, HBM) for a in (gains, place, node_part, node_first, node_second, grad_nodes, node_feat)),
        ],
        [
            (VMEM, rows_bf16, BF16),
            (VMEM, rows_bf16, BF16),
            (VMEM, rows_bf16, BF16),
            (VMEM, (edges, 128), F32),
            (VMEM, nodes_f32, BF16),
            (VMEM, (1, width), F32),
            (VMEM, (chips, share, width), BF16),
            (HBM, nodes_f32, F32),
            (HBM, (chips, share, width), BF16),
        ],
        [
            VMEM(gains.shape, F32),
            VMEM((nodes, edges), BF16),
            VMEM(nodes_f32, F32),
            VMEM(node_first.shape, BF16),
            VMEM(node_second.shape, BF16),
            VMEM(nodes_f32, BF16),
            VMEM(nodes_f32, BF16),
            VMEM(rows_bf16, BF16),
            VMEM(node_first.shape, F32),
            VMEM(node_second.shape, F32),
            VMEM(nodes_f32, F32),
            VMEM((chips, share, width), BF16),
            semaphores(7),
            semaphores(chips),
            semaphores(1),
        ],
        flops=block * (2 * edges + 9 * nodes),
    )
    node_received = lax.ppermute(node_send, "space", other_core)

    share = edge_first.shape[0] // devices + edge_second.shape[0] // devices
    back_shape = (devices, capacity + 8, width)
    edge_keep, node_total, grad_edge_feat, back, edge_send = call(
        backward_kernel,
        "backward",
        [
            (live_blocks, SMEM),
            *(
                (a, VMEM)
                for a in (
                    grad_edges,
                    slope,
                    hidden,
                    normed,
                    inv_std,
                    grad_agg,
                    node_gain,
                    halo,
                    second,
                    receive,
                    edge_first,
                    gains,
                )
            ),
            *((a, HBM) for a in (place, edge_feat, node_feat, node_base)),
        ],
        [
            (VMEM, (chips, share, width), BF16),
            (HBM, nodes_f32, F32),
            (HBM, rows_bf16, BF16),
            (HBM, back_shape, BF16),
            (HBM, (chips, share, width), BF16),
        ],
        [
            VMEM(place_shape, BF16),
            VMEM(rows_bf16, BF16),
            VMEM(nodes_f32, BF16),
            VMEM(nodes_f32, F32),
            VMEM(rows_bf16, BF16),
            VMEM(rows_bf16, BF16),
            VMEM(rows_bf16, BF16),
            VMEM(back_shape, BF16),
            VMEM(edge_first.shape, F32),
            VMEM(edge_second.shape, F32),
            VMEM((chips, share, width), BF16),
            semaphores(chips),
            semaphores(edges // CHUNK),
            semaphores(2),
            semaphores(4),
        ],
        flops=block * (6 * edges),
    )

    edge_received = lax.ppermute(edge_send, "space", other_core)
    halves = (node_keep, node_received, edge_keep, edge_received)
    orders = exchange_orders(chips)
    bits = [order[0] for order in orders]
    shape = (chips // 2, node_keep.shape[1] + edge_keep.shape[1], width // 2)
    sent, kept = fold_call(functools.partial(first_fold_kernel, bits), "first_fold", halves, shape)
    received = exchange(sent, bits, devices)
    returned = lax.all_to_all(back, "space", split_axis=0, concat_axis=0, tiled=True)
    for done in range(1, len(orders[0])):
        bits = [order[done] for order in orders]
        positions = [
            bit - sum(earlier < bit for earlier in order[:done]) for bit, order in zip(bits, orders)
        ]
        shape = (shape[0] // 2, *shape[1:])
        sent, kept = fold_call(
            functools.partial(later_fold_kernel, bits, positions), "later_fold", (*kept, *received), shape
        )
        received = exchange(sent, bits, devices)

    grad_node_feat, gain_totals = call(
        nodes_kernel,
        "nodes",
        [(node_total, HBM), (returned, VMEM), (send_table, HBM)],
        [(HBM, (nodes, width), BF16), (HBM, (2, width), F32)],
        [VMEM((nodes, width), F32), VMEM(send_table.shape, INT), VMEM((nodes, width), BF16), VMEM((2, width), F32), semaphores(2)],
    )
    shapes = [(w.shape[0] // devices, width) for w in (node_first, node_second, edge_first, edge_second)]
    grad_node_first, grad_node_second, grad_edge_first, grad_edge_second = call(
        shares_kernel,
        "shares",
        [(a, VMEM) for a in (*kept, *received)],
        [(HBM, shape, F32) for shape in shapes],
        [*(VMEM(shape, F32) for shape in shapes), semaphores(4)],
    )
    return (
        grad_node_feat,
        grad_edge_feat,
        grad_edge_first,
        grad_edge_second,
        grad_node_first,
        grad_node_second,
        gain_totals,
    )


def solution(mesh):
    placed = (
        P(("group", "space"), None),
        P(("group", "space"), None),
        P(("group", "space"), None),
        P(("group", "space"), None),
        P(),
        P(),
        P(),
        P(),
        P(),
        P(("group", "space")),
        P(("group", "space")),
        P(("group", "space")),
        P(("group", "space"), None, None),
        P(("group", "space")),
    )
    return jax.shard_map(
        shards,
        mesh=mesh,
        in_specs=placed,
        out_specs=(
            P(("group", "space"), None),
            P(("group", "space"), None),
            P(("group", "space"), None),
            P(("group", "space"), None),
            P(("group", "space"), None),
            P(("group", "space"), None),
            P("group", None),
        ),
        check_vma=False,
    )
```

```python
import functools

import jax
import jax.numpy as jnp
from jax import lax
from jax.experimental import pallas as pl
from jax.experimental.pallas import tpu as pltpu
from jax.sharding import PartitionSpec as P

EDGE_BLOCK = 128
CHUNK = 512
GAIN_ROWS = 16
EPS = 1e-05
BF16 = jnp.bfloat16
F32 = jnp.float32
INT = jnp.int32
MIB = 1 << 20


def dot(left, right):
    return lax.dot_general(left, right, (((1,), (0,)), ((), ())), preferred_element_type=F32)


def times_transposed(left, right):
    return lax.dot_general(left, right, (((1,), (1,)), ((), ())), preferred_element_type=F32)


def transposed_times(left, right):
    return lax.dot_general(left, right, (((0,), (0,)), ((), ())), preferred_element_type=F32)


def ones_where(mask):
    return jnp.where(mask, 1.0, 0.0).astype(BF16)


def chosen(row, width):
    lane = lax.broadcasted_iota(INT, (EDGE_BLOCK, EDGE_BLOCK), 1)
    col = jnp.transpose(jnp.broadcast_to(row, (EDGE_BLOCK, EDGE_BLOCK)))
    return jnp.concatenate(
        [ones_where(col == lane + EDGE_BLOCK * j) for j in range(width // EDGE_BLOCK)], axis=1
    )


def chosen_transposed(row, width):
    return ones_where(lax.broadcasted_iota(INT, (width, EDGE_BLOCK), 0) == row)


def send_choice(table_ref, node_rows):
    capacity, devices = table_ref.shape[1:]
    lane = lax.broadcasted_iota(INT, (capacity, node_rows), 1)
    table = table_ref[0]
    out = [jnp.where(table[:, j : j + 1] == lane, 1.0, 0.0) for j in range(devices)]
    return jnp.concatenate(out, axis=0).astype(BF16)


def activation(pre):
    sigmoid = 0.5 * jnp.tanh(0.5 * pre) + 0.5
    hidden = pre * sigmoid
    return hidden.astype(BF16), sigmoid + hidden * (1.0 - sigmoid)


def normalize(post):
    centred = post - jnp.mean(post, axis=-1, keepdims=True)
    inv_std = lax.rsqrt(jnp.mean(centred * centred, axis=-1, keepdims=True) + EPS)
    return centred * inv_std, inv_std


def grad_normalize(grad_out, gain, normed, inv_std):
    grad_normed = grad_out * gain
    return (
        inv_std
        * (
            grad_normed
            - jnp.mean(grad_normed, axis=-1, keepdims=True)
            - normed * jnp.mean(grad_normed * normed, axis=-1, keepdims=True)
        )
    ).astype(BF16)


def pack(keep_ref, send_ref, stage, sems, sources, tail):
    chips = stage.shape[0]
    core = lax.rem(lax.axis_index("space"), 2)
    copies = []
    for away in (True, False):
        for k in range(chips):
            place = 2 * k + 1 - core if away else 2 * k + core
            pieces = []
            for source in sources:
                share = source.shape[0] // (2 * chips)
                pieces.append(source[pl.ds(pl.multiple_of(place * share, 8), share), :])
            rows = jnp.concatenate([*pieces, *tail], axis=0).astype(BF16)
            if away:
                stage[k] = rows
                copies.append(pltpu.make_async_copy(stage.at[k], send_ref.at[k], sems.at[k]))
                copies[-1].start()
            else:
                keep_ref[k] = rows
    return copies


def weight_grads(columns, acts, grads, outs, sums, tail=()):
    place, edge, node, halo, hidden, aggregate, node_hidden = acts
    grad_pre, grad_post, node_grad_pre, node_grad_post = grads
    placed_ref, keep_ref, send_ref, stage, sems = outs
    node_first, node_second, edge_first, edge_second = sums
    nodes, width = node.shape
    far_end = place.shape[0] - nodes
    pre = grad_pre[:, columns]
    placed = dot(place[...], pre).astype(BF16)
    placed_ref[...] = placed
    edge_second[...] = transposed_times(hidden[...], grad_post[:, columns])
    edge_first[2 * width :] = transposed_times(edge[...], pre)
    node_first[0:width] = transposed_times(node[...], node_grad_pre[:, columns])
    node_first[width:] = transposed_times(aggregate[...], node_grad_pre[:, columns])
    node_second[...] = transposed_times(node_hidden[...], node_grad_post[:, columns])
    edge_first[0:width] = transposed_times(node[...], placed[0:nodes]) + transposed_times(
        halo[...], placed[nodes:far_end]
    )
    edge_first[width : 2 * width] = transposed_times(node[...], placed[far_end:])
    return pack(keep_ref, send_ref, stage, sems, sums, tail)


def outgoing_kernel(node_hbm, table_hbm, out_ref, node, table, stage, sems):
    copies = [
        pltpu.make_async_copy(node_hbm, node, sems.at[0]),
        pltpu.make_async_copy(table_hbm, table, sems.at[1]),
    ]
    for copy in copies:
        copy.start()
    copies[1].wait()
    choice = send_choice(table, node.shape[0])
    copies[0].wait()
    stage[...] = dot(choice, node[...]).astype(BF16)
    copy = pltpu.make_async_copy(stage, out_ref, sems.at[0])
    copy.start()
    copy.wait()


def load(sources, targets, sems):
    copies = [
        pltpu.make_async_copy(source, target, sems.at[k])
        for k, (source, target) in enumerate(zip(sources, targets))
    ]
    for copy in copies:
        copy.start()
    return copies


def prepare_kernel(
    live_ref,
    peer_hbm,
    slot_hbm,
    recv_hbm,
    node_hbm,
    first_hbm,
    edge_hbm,
    node_first_hbm,
    second_hbm,
    part_ref,
    far_ref,
    top_ref,
    second_ref,
    node_part_ref,
    receive_ref,
    place_ref,
    peer_ref,
    slot_ref,
    recv_ref,
    node,
    first,
    edge,
    node_first,
    node_part,
    receive,
    places,
    table,
    sems,
    out_sems,
):
    nodes, width = node.shape
    copies = load(
        (
            peer_hbm,
            slot_hbm,
            recv_hbm,
            node_hbm,
            first_hbm,
            edge_hbm,
            node_first_hbm.at[pl.ds(0, width)],
            second_hbm,
            first_hbm.at[pl.ds(0, width)],
        ),
        (peer_ref, slot_ref, recv_ref, node, first, edge, node_first, second_ref, top_ref),
        sems,
    )
    own = lax.axis_index("space")
    blocks = peer_ref.shape[0]
    halo_rows = far_ref.shape[1]
    capacity = halo_rows // lax.axis_size("space")
    for k in range(3):
        copies[k].wait()
    near = []
    for b in range(blocks):
        rows = pl.ds(b * EDGE_BLOCK, EDGE_BLOCK)
        peer, slot, recv = (ref[b : b + 1, :] for ref in (peer_ref, slot_ref, recv_ref))
        mine = peer == own
        far = peer * capacity + slot
        near.append(chosen(jnp.where(mine, slot, -1), nodes))
        far_ref[rows, :] = chosen(jnp.where(mine, -1, far), halo_rows)
        received = jnp.where(b < live_ref[0], recv, -1)
        receive[rows, :] = chosen(received, nodes)
        places[0 : nodes + halo_rows, rows] = chosen_transposed(
            jnp.where(mine, slot, nodes + far), nodes + halo_rows
        )
        places[nodes + halo_rows :, rows] = chosen_transposed(received, nodes)
    out_copies = load((receive, places), (receive_ref, place_ref), out_sems)
    copies[3].wait()
    copies[4].wait()
    table[0:nodes] = dot(node[...], first[0:width]).astype(BF16)
    table[nodes:] = dot(node[...], first[width : 2 * width]).astype(BF16)
    copies[5].wait()
    count = CHUNK // EDGE_BLOCK
    for c in range(blocks // count):
        rows = pl.ds(c * CHUNK, CHUNK)
        choice = jnp.concatenate(
            [jnp.concatenate(near[c * count : (c + 1) * count], axis=0), receive[rows, :]], axis=1
        )
        part_ref[rows, :] = dot(edge[rows, :], first[2 * width :]) + dot(choice, table[...])
    copies[6].wait()
    node_part[...] = dot(node[...], node_first[...])
    out_copies.append(pltpu.make_async_copy(node_part, node_part_ref, out_sems.at[2]))
    out_copies[2].start()
    for copy in (*copies[7:], *out_copies):
        copy.wait()


def forward_kernel(
    part_ref,
    halo_ref,
    far_ref,
    top_ref,
    second_ref,
    gains_hbm,
    place_hbm,
    node_part_hbm,
    node_first_hbm,
    node_second_hbm,
    grad_nodes_hbm,
    slope_ref,
    hidden_ref,
    normed_ref,
    inv_ref,
    grad_agg_ref,
    node_gain_ref,
    aggregate_ref,
    node_hidden_ref,
    node_grad_pre_ref,
    node_grad_post_ref,
    gains,
    place,
    node_part,
    node_first,
    node_second,
    grad_nodes,
    messages,
    sems,
):
    nodes, width = node_part.shape
    copies = load(
        (
            gains_hbm,
            place_hbm.at[pl.ds(place_hbm.shape[0] - nodes, nodes)],
            node_part_hbm,
            node_first_hbm.at[pl.ds(width, width)],
            node_second_hbm,
            grad_nodes_hbm,
        ),
        (gains, place, node_part, node_first, node_second, grad_nodes),
        sems,
    )
    halo_part = dot(halo_ref[...], top_ref[...]).astype(BF16)
    for c in range(part_ref.shape[0] // CHUNK):
        rows = pl.ds(c * CHUNK, CHUNK)
        hidden, slope = activation(part_ref[rows, :] + dot(far_ref[rows, :], halo_part))
        hidden_ref[rows, :] = hidden
        slope_ref[rows, :] = slope.astype(BF16)
        normed, inv_std = normalize(dot(hidden, second_ref[...]))
        normed_ref[rows, :] = normed.astype(BF16)
        inv_ref[rows, :] = jnp.broadcast_to(inv_std, (CHUNK, inv_ref.shape[1]))
        if c == 0:
            copies[0].wait()
        messages[rows, :] = (normed * gains[0:1]).astype(BF16)
    for copy in copies[1:]:
        copy.wait()
    aggregate = dot(place[...], messages[...]).astype(BF16)
    node_hidden, node_slope = activation(node_part[...] + dot(aggregate, node_first[...]))
    node_normed, node_inv = normalize(dot(node_hidden, node_second[...]))
    grad_out = grad_nodes[...].astype(F32)
    node_gain_ref[...] = jnp.sum(grad_out * node_normed, axis=0, keepdims=True)
    grad_post = grad_normalize(grad_out, gains[1:2], node_normed, node_inv)
    grad_pre = (times_transposed(grad_post, node_second[...]) * node_slope).astype(BF16)
    grad_agg_ref[...] = times_transposed(grad_pre, node_first[...]).astype(BF16)
    aggregate_ref[...] = aggregate
    node_hidden_ref[...] = node_hidden
    node_grad_pre_ref[...] = grad_pre
    node_grad_post_ref[...] = grad_post


def backward_kernel(
    live_ref,
    grad_edges_ref,
    slope_ref,
    hidden_ref,
    normed_ref,
    inv_ref,
    grad_agg_ref,
    node_gain_ref,
    aggregate_ref,
    node_hidden_ref,
    node_grad_pre_ref,
    node_grad_post_ref,
    halo_ref,
    second_ref,
    receive_ref,
    gains_ref,
    place_hbm,
    edge_hbm,
    node_hbm,
    grad_post_ref,
    grad_pre_ref,
    placed_ref,
    keep_ref,
    send_ref,
    place,
    edge,
    node,
    node_first,
    node_second,
    edge_first,
    edge_second,
    stage,
    sems,
    load_sems,
):
    width = node.shape[1]
    half = placed_ref.shape[1]
    loads = load((place_hbm, edge_hbm, node_hbm), (place, edge, node), load_sems)
    count = CHUNK // EDGE_BLOCK
    grad_gain = jnp.zeros((1, width), F32)
    for c in range(edge.shape[0] // CHUNK):
        rows = pl.ds(c * CHUNK, CHUNK)
        live = jnp.concatenate(
            [
                jnp.where(jnp.full((EDGE_BLOCK, 1), c * count + k, INT) < live_ref[0], 1.0, 0.0)
                for k in range(count)
            ],
            axis=0,
        )
        grad_out = grad_edges_ref[rows, :].astype(F32) * live + dot(receive_ref[rows, :], grad_agg_ref[...])
        normed = normed_ref[rows, :].astype(F32)
        grad_gain += jnp.sum(grad_out * normed, axis=0, keepdims=True)
        grad_post = grad_normalize(grad_out, gains_ref[0:1], normed, inv_ref[rows, 0:1])
        grad_post_ref[rows, :] = grad_post
        grad_hidden = times_transposed(grad_post, second_ref[...])
        grad_pre_ref[rows, :] = (grad_hidden * slope_ref[rows, :].astype(F32)).astype(BF16)
    for copy in loads:
        copy.wait()
    node_gain = node_gain_ref[...]
    tail = [row[:, half * k : half * (k + 1)] for row in (grad_gain, node_gain) for k in range(2)]
    copies = weight_grads(
        slice(0, half),
        (place, edge, node, halo_ref, hidden_ref, aggregate_ref, node_hidden_ref),
        (grad_pre_ref, grad_post_ref, node_grad_pre_ref, node_grad_post_ref),
        (placed_ref, keep_ref, send_ref, stage, sems),
        (node_first, node_second, edge_first, edge_second),
        [*tail, jnp.zeros((GAIN_ROWS - 4, half), F32)],
    )
    for copy in copies:
        copy.wait()


def right_kernel(
    grad_post_ref,
    grad_pre_ref,
    hidden_ref,
    aggregate_ref,
    node_hidden_ref,
    node_grad_pre_ref,
    node_grad_post_ref,
    halo_ref,
    place_ref,
    edge_ref,
    node_ref,
    placed_ref,
    keep_ref,
    send_ref,
    node_first,
    node_second,
    edge_first,
    edge_second,
    stage,
    sems,
):
    half = placed_ref.shape[1]
    copies = weight_grads(
        slice(half, 2 * half),
        (place_ref, edge_ref, node_ref, halo_ref, hidden_ref, aggregate_ref, node_hidden_ref),
        (grad_pre_ref, grad_post_ref, node_grad_pre_ref, node_grad_post_ref),
        (placed_ref, keep_ref, send_ref, stage, sems),
        (node_first, node_second, edge_first, edge_second),
    )
    for copy in copies:
        copy.wait()


def finish_kernel(
    left_ref,
    right_ref,
    grad_pre_ref,
    node_grad_pre_ref,
    first_hbm,
    node_first_hbm,
    grad_nodes_hbm,
    grad_edges_hbm,
    back_ref,
    edge_out_ref,
    node_total_ref,
    first,
    node_first,
    grad_nodes,
    grad_edges,
    back_stage,
    edge_out,
    node_total,
    sems,
    out_sems,
    edge_sems,
):
    nodes, width = grad_nodes.shape
    loads = load(
        (first_hbm, node_first_hbm.at[pl.ds(0, width)], grad_nodes_hbm, grad_edges_hbm),
        (first, node_first, grad_nodes, grad_edges),
        sems,
    )
    devices, capacity = back_ref.shape[:2]
    far_end = left_ref.shape[0] - nodes
    placed = jnp.concatenate([left_ref[...], right_ref[...]], axis=1)
    loads[0].wait()
    back = times_transposed(placed[nodes:far_end], first[0:width])
    for k in range(devices):
        back_stage[k] = back[k * capacity : (k + 1) * capacity].astype(BF16)
    copies = load((back_stage,), (back_ref,), out_sems)
    loads[1].wait()
    loads[2].wait()
    node_total[...] = (
        grad_nodes[...].astype(F32)
        + times_transposed(node_grad_pre_ref[...], node_first[...])
        + times_transposed(placed[0:nodes], first[0:width])
        + times_transposed(placed[far_end:], first[width : 2 * width])
    )
    copies.append(pltpu.make_async_copy(node_total, node_total_ref, out_sems.at[1]))
    copies[-1].start()
    loads[3].wait()
    for c in range(grad_edges.shape[0] // CHUNK):
        rows = pl.ds(c * CHUNK, CHUNK)
        grad_edge = grad_edges[rows, :].astype(F32) + times_transposed(grad_pre_ref[rows, :], first[2 * width :])
        edge_out[rows, :] = grad_edge.astype(BF16)
        copies.append(pltpu.make_async_copy(edge_out.at[rows], edge_out_ref.at[rows], edge_sems.at[c]))
        copies[-1].start()
    for copy in copies:
        copy.wait()


def nodes_kernel(total_hbm, returned_ref, table_hbm, out_ref, total, table, stage, sems):
    loads = load((total_hbm, table_hbm), (total, table), sems)
    capacity, devices = table.shape[1:]
    returned = jnp.concatenate([returned_ref[k].astype(F32) for k in range(devices)], axis=0).astype(BF16)
    for copy in loads:
        copy.wait()
    choice = send_choice(table, total.shape[0])
    stage[...] = (total[...] + transposed_times(choice, returned)).astype(BF16)
    copy = pltpu.make_async_copy(stage, out_ref, sems.at[0])
    copy.start()
    copy.wait()


def exchange_orders(chips):
    bits = list(range(chips.bit_length() - 1))
    return bits, [*bits[1::-1], *bits[2:]]


def exchange(piece, bit, devices):
    return lax.ppermute(piece, "space", [(i, i ^ (2 << bit)) for i in range(devices)])


def half_of(step, bit, position, away):
    value = (lax.axis_index("space") >> (bit + 1)) & 1
    value = 1 - value if away else value
    low = step & ((1 << position) - 1)
    return ((step >> position) << (position + 1)) | (value << position) | low


def fold_kernel(bit, position, kept_ref, received_ref, *refs):
    sent, kept, stage, sems = refs[-4:]
    copies = []
    for away in (True, False):
        for k in range(kept.shape[0]):
            place = half_of(k, bit, position, away)
            block = (kept_ref[place].astype(F32) + received_ref[place].astype(F32)).astype(BF16)
            if away:
                stage[k] = block
                copies.append(pltpu.make_async_copy(stage.at[k], sent.at[k], sems.at[k]))
                copies[-1].start()
            else:
                kept[k] = block
    for copy in copies:
        copy.wait()


def shares_kernel(left, left_in, right, right_in, *refs):
    outs, stages, sems = refs[:5], refs[5:10], refs[10]
    sides = [a[0].astype(F32) + b[0].astype(F32) for a, b in ((left, left_in), (right, right_in))]
    rows = sides[1].shape[0]
    total = jnp.concatenate([sides[0][0:rows], sides[1]], axis=1)
    start = 0
    for out, stage in zip(outs[:4], stages):
        stage[...] = total[start : start + out.shape[0]]
        start += out.shape[0]
    gains = [sides[0][rows + k : rows + k + 1] for k in range(4)]
    stages[4][...] = jnp.concatenate(
        [jnp.concatenate(gains[0:2], axis=1), jnp.concatenate(gains[2:4], axis=1)], axis=0
    )
    for copy in load(stages, outs, sems):
        copy.wait()


VMEM, HBM, SMEM = pltpu.VMEM, pltpu.HBM, pltpu.SMEM


def call(body, name, operands, outs, scratch=(), flops=0):
    spaces = [space for _, space in operands]
    arrays = [
        array if space is SMEM else pltpu.with_memory_space_constraint(array, space) for array, space in operands
    ]
    moved = sum(a.size * a.dtype.itemsize for a, _ in operands)
    return pl.pallas_call(
        body,
        in_specs=[pl.BlockSpec(memory_space=space) for space in spaces],
        out_specs=[pl.BlockSpec(memory_space=space) for space, _, _ in outs],
        out_shape=[space(shape, dtype) for space, shape, dtype in outs],
        scratch_shapes=scratch,
        name=name,
        cost_estimate=pl.CostEstimate(flops=flops, bytes_accessed=moved, transcendentals=0),
        compiler_params=pltpu.CompilerParams(vmem_limit_bytes=24 * MIB),
    )(*arrays)


def semaphores(count):
    return pltpu.SemaphoreType.DMA((count,))


def fold_call(name, bit, position, kept, received, *before):
    shape = (kept.shape[0] // 2, *kept.shape[1:])
    return call(
        functools.partial(fold_kernel, bit, position),
        name,
        [(kept, VMEM), (received, VMEM), *((a, HBM) for a in before)],
        [(HBM, shape, BF16), (VMEM, shape, BF16)],
        [VMEM(shape, BF16), semaphores(shape[0])],
    )


def shards(
    node_feat,
    edge_feat,
    grad_nodes,
    grad_edges,
    edge_first,
    edge_second,
    node_first,
    node_second,
    gains,
    edge_peer,
    edge_slot,
    edge_recv,
    send_index,
    live_blocks,
):
    nodes, width = node_feat.shape
    edges = edge_feat.shape[0]
    devices, capacity = send_index.shape[1:]
    chips = devices // 2
    halo_rows = devices * capacity
    peer, slot, recv = (a.reshape(edges // EDGE_BLOCK, EDGE_BLOCK) for a in (edge_peer, edge_slot, edge_recv))
    other_core = [(i, i ^ 1) for i in range(devices)]
    block = width * width * 2

    send_table = jnp.swapaxes(send_index, 1, 2)
    (outgoing,) = call(
        outgoing_kernel,
        "outgoing",
        [(node_feat, HBM), (send_table, HBM)],
        [(HBM, (halo_rows, width), BF16)],
        [
            VMEM(node_feat.shape, BF16),
            VMEM(send_table.shape, INT),
            VMEM((halo_rows, width), BF16),
            semaphores(2),
        ],
    )
    halo = lax.all_to_all(
        outgoing.reshape(devices, capacity, width), "space", split_axis=0, concat_axis=0, tiled=True
    ).reshape(halo_rows, width)

    rows_bf16, nodes_f32 = (edges, width), (nodes, width)
    top_shape, place_shape = (width, width), (2 * nodes + halo_rows, edges)
    part, far, top, second, node_part, receive, place = call(
        prepare_kernel,
        "prepare",
        [
            (live_blocks, SMEM),
            *(
                (a, HBM)
                for a in (peer, slot, recv, node_feat, edge_first, edge_feat, node_first, edge_second)
            ),
        ],
        [
            (VMEM, rows_bf16, F32),
            (VMEM, (edges, halo_rows), BF16),
            (VMEM, top_shape, BF16),
            (VMEM, edge_second.shape, BF16),
            (HBM, nodes_f32, F32),
            (HBM, (edges, nodes), BF16),
            (HBM, place_shape, BF16),
        ],
        [
            VMEM(peer.shape, INT),
            VMEM(slot.shape, INT),
            VMEM(recv.shape, INT),
            VMEM(node_feat.shape, BF16),
            VMEM(edge_first.shape, BF16),
            VMEM(edge_feat.shape, BF16),
            VMEM(top_shape, BF16),
            VMEM(nodes_f32, F32),
            VMEM((edges, nodes), BF16),
            VMEM(place_shape, BF16),
            VMEM((2 * nodes, width), BF16),
            semaphores(9),
            semaphores(3),
        ],
        flops=block * (2 * edges + 3 * nodes),
    )

    nodes_bf16 = (VMEM, nodes_f32, BF16)
    kept_rows = (VMEM, rows_bf16, BF16)
    (
        slope,
        hidden,
        normed,
        inv_std,
        grad_agg,
        node_gain,
        aggregate,
        node_hidden,
        node_grad_pre,
        node_grad_post,
    ) = call(
        forward_kernel,
        "forward",
        [
            *((a, VMEM) for a in (part, halo, far, top, second)),
            *((a, HBM) for a in (gains, place, node_part, node_first, node_second, grad_nodes)),
        ],
        [
            kept_rows,
            kept_rows,
            kept_rows,
            (VMEM, (edges, 128), F32),
            nodes_bf16,
            (VMEM, (1, width), F32),
            nodes_bf16,
            nodes_bf16,
            nodes_bf16,
            nodes_bf16,
        ],
        [
            VMEM(gains.shape, F32),
            VMEM((nodes, edges), BF16),
            VMEM(nodes_f32, F32),
            VMEM(top_shape, BF16),
            VMEM(node_second.shape, BF16),
            VMEM(nodes_f32, BF16),
            VMEM(rows_bf16, BF16),
            semaphores(6),
        ],
        flops=block * (2 * edges + 6 * nodes),
    )

    half = width // 2
    weights = (node_first, node_second, edge_first, edge_second)
    share = sum(w.shape[0] // devices for w in weights)
    left_shape, right_shape = (chips, share + GAIN_ROWS, half), (chips, share, half)
    placed = (VMEM, (2 * nodes + halo_rows, half), BF16)
    halves = [VMEM((w.shape[0], half), F32) for w in weights]
    grad_post, grad_pre, left_placed, left_keep, left_send = call(
        backward_kernel,
        "backward",
        [
            (live_blocks, SMEM),
            *(
                (a, VMEM)
                for a in (
                    grad_edges,
                    slope,
                    hidden,
                    normed,
                    inv_std,
                    grad_agg,
                    node_gain,
                    aggregate,
                    node_hidden,
                    node_grad_pre,
                    node_grad_post,
                    halo,
                    second,
                    receive,
                    gains,
                )
            ),
            *((a, HBM) for a in (place, edge_feat, node_feat)),
        ],
        [kept_rows, kept_rows, placed, (VMEM, left_shape, BF16), (HBM, left_shape, BF16)],
        [
            VMEM(place_shape, BF16),
            VMEM(rows_bf16, BF16),
            VMEM(nodes_f32, BF16),
            *halves,
            VMEM(left_shape, BF16),
            semaphores(chips),
            semaphores(3),
        ],
        flops=block * (4 * edges),
    )
    left_received = lax.ppermute(left_send, "space", other_core)
    right_placed, right_keep, right_send = call(
        right_kernel,
        "right",
        [
            (a, VMEM)
            for a in (
                grad_post,
                grad_pre,
                hidden,
                aggregate,
                node_hidden,
                node_grad_pre,
                node_grad_post,
                halo,
                place,
                edge_feat,
                node_feat,
            )
        ],
        [placed, (VMEM, right_shape, BF16), (HBM, right_shape, BF16)],
        [*halves, VMEM(right_shape, BF16), semaphores(chips)],
        flops=block * (2 * edges),
    )
    right_received = lax.ppermute(right_send, "space", other_core)
    back, grad_edge_feat, node_total = call(
        finish_kernel,
        "finish",
        [
            *((a, VMEM) for a in (left_placed, right_placed, grad_pre, node_grad_pre)),
            *((a, HBM) for a in (edge_first, node_first, grad_nodes, grad_edges)),
        ],
        [
            (HBM, (devices, capacity, width), BF16),
            (HBM, rows_bf16, BF16),
            (HBM, nodes_f32, F32),
        ],
        [
            VMEM(edge_first.shape, BF16),
            VMEM(top_shape, BF16),
            VMEM(nodes_f32, BF16),
            VMEM(rows_bf16, BF16),
            VMEM((devices, capacity, width), BF16),
            VMEM(rows_bf16, BF16),
            VMEM(nodes_f32, F32),
            semaphores(4),
            semaphores(2),
            semaphores(edges // CHUNK),
        ],
        flops=block * (edges + 4 * nodes),
    )
    returned = lax.all_to_all(back, "space", split_axis=0, concat_axis=0, tiled=True)

    pieces = [("left", left_keep, left_received), ("right", right_keep, right_received)]
    for stage in range(chips.bit_length() - 1):
        for side, order in enumerate(exchange_orders(chips)):
            name, kept, received = pieces[side]
            bit = order[stage]
            position = bit - sum(earlier < bit for earlier in order[:stage])
            before = (back,) if stage == 1 and side == 0 else ()
            sent, kept = fold_call(f"{name}_fold", bit, position, kept, received, *before)
            pieces[side] = (name, kept, exchange(sent, bit, devices))

    (grad_node_feat,) = call(
        nodes_kernel,
        "nodes",
        [(node_total, HBM), (returned, VMEM), (send_table, HBM)],
        [(HBM, nodes_f32, BF16)],
        [VMEM(nodes_f32, F32), VMEM(send_table.shape, INT), VMEM(nodes_f32, BF16), semaphores(2)],
    )
    shapes = [*((w.shape[0] // devices, width) for w in weights), (2, width)]
    grad_node_first, grad_node_second, grad_edge_first, grad_edge_second, gain_totals = call(
        shares_kernel,
        "shares",
        [(a, VMEM) for _, *pair in pieces for a in pair],
        [(HBM, shape, F32) for shape in shapes],
        [*(VMEM(shape, F32) for shape in shapes), semaphores(5)],
    )
    return (
        grad_node_feat,
        grad_edge_feat,
        grad_edge_first,
        grad_edge_second,
        grad_node_first,
        grad_node_second,
        gain_totals,
    )


def solution(mesh):
    placed = (
        P(("group", "space"), None),
        P(("group", "space"), None),
        P(("group", "space"), None),
        P(("group", "space"), None),
        P(),
        P(),
        P(),
        P(),
        P(),
        P(("group", "space")),
        P(("group", "space")),
        P(("group", "space")),
        P(("group", "space"), None, None),
        P(("group", "space")),
    )
    return jax.shard_map(
        shards,
        mesh=mesh,
        in_specs=placed,
        out_specs=(
            P(("group", "space"), None),
            P(("group", "space"), None),
            P(("group", "space"), None),
            P(("group", "space"), None),
            P(("group", "space"), None),
            P(("group", "space"), None),
            P("group", None),
        ),
        check_vma=False,
    )
```

```python
import functools

import jax
import jax.numpy as jnp
from jax import lax
from jax.experimental import pallas as pl
from jax.experimental.pallas import tpu as pltpu
from jax.sharding import PartitionSpec as P

EDGE_BLOCK = 128
CHUNK = 512
GAIN_ROWS = 16
EPS = 1e-05
BF16 = jnp.bfloat16
F32 = jnp.float32
INT = jnp.int32
MIB = 1 << 20


def dot(left, right):
    return lax.dot_general(left, right, (((1,), (0,)), ((), ())), preferred_element_type=F32)


def times_transposed(left, right):
    return lax.dot_general(left, right, (((1,), (1,)), ((), ())), preferred_element_type=F32)


def transposed_times(left, right):
    return lax.dot_general(left, right, (((0,), (0,)), ((), ())), preferred_element_type=F32)


def ones_where(mask):
    return jnp.where(mask, 1.0, 0.0).astype(BF16)


def chosen(row, width):
    lane = lax.broadcasted_iota(INT, (EDGE_BLOCK, EDGE_BLOCK), 1)
    col = jnp.transpose(jnp.broadcast_to(row, (EDGE_BLOCK, EDGE_BLOCK)))
    return jnp.concatenate(
        [ones_where(col == lane + EDGE_BLOCK * j) for j in range(width // EDGE_BLOCK)], axis=1
    )


def chosen_transposed(row, width):
    return ones_where(lax.broadcasted_iota(INT, (width, EDGE_BLOCK), 0) == row)


def send_choice(table_ref, node_rows):
    capacity, devices = table_ref.shape[1:]
    lane = lax.broadcasted_iota(INT, (capacity, node_rows), 1)
    table = table_ref[0]
    out = [jnp.where(table[:, j : j + 1] == lane, 1.0, 0.0) for j in range(devices)]
    return jnp.concatenate(out, axis=0).astype(BF16)


def activation(pre):
    sigmoid = 0.5 * jnp.tanh(0.5 * pre) + 0.5
    hidden = pre * sigmoid
    return hidden.astype(BF16), sigmoid + hidden * (1.0 - sigmoid)


def normalize(post):
    centred = post - jnp.mean(post, axis=-1, keepdims=True)
    inv_std = lax.rsqrt(jnp.mean(centred * centred, axis=-1, keepdims=True) + EPS)
    return centred * inv_std, inv_std


def grad_normalize(grad_out, gain, normed, inv_std):
    grad_normed = grad_out * gain
    return (
        inv_std
        * (
            grad_normed
            - jnp.mean(grad_normed, axis=-1, keepdims=True)
            - normed * jnp.mean(grad_normed * normed, axis=-1, keepdims=True)
        )
    ).astype(BF16)


def pack(keep_ref, send_ref, stage, sems, sources, tail):
    chips = stage.shape[0]
    core = lax.rem(lax.axis_index("space"), 2)
    copies = []
    for away in (True, False):
        for k in range(chips):
            place = 2 * k + 1 - core if away else 2 * k + core
            pieces = []
            for source in sources:
                share = source.shape[0] // (2 * chips)
                pieces.append(source[pl.ds(pl.multiple_of(place * share, 8), share), :])
            rows = jnp.concatenate([*pieces, *tail], axis=0).astype(BF16)
            if away:
                stage[k] = rows
                copies.append(pltpu.make_async_copy(stage.at[k], send_ref.at[k], sems.at[k]))
                copies[-1].start()
            else:
                keep_ref[k] = rows
    return copies


def weight_grads(columns, acts, grads, outs, sums, tail=()):
    place, edge, node, halo, hidden, aggregate, node_hidden = acts
    grad_pre, grad_post, node_grad_pre, node_grad_post = grads
    placed_ref, keep_ref, send_ref, stage, sems = outs
    node_first, node_second, edge_first, edge_second = sums
    nodes, width = node.shape
    far_end = place.shape[0] - nodes
    pre = grad_pre[:, columns]
    placed = dot(place[...], pre).astype(BF16)
    placed_ref[...] = placed
    edge_second[...] = transposed_times(hidden[...], grad_post[:, columns])
    edge_first[2 * width :] = transposed_times(edge[...], pre)
    node_first[0:width] = transposed_times(node[...], node_grad_pre[:, columns])
    node_first[width:] = transposed_times(aggregate[...], node_grad_pre[:, columns])
    node_second[...] = transposed_times(node_hidden[...], node_grad_post[:, columns])
    edge_first[0:width] = transposed_times(node[...], placed[0:nodes]) + transposed_times(
        halo[...], placed[nodes:far_end]
    )
    edge_first[width : 2 * width] = transposed_times(node[...], placed[far_end:])
    return pack(keep_ref, send_ref, stage, sems, sums, tail)


def outgoing_kernel(node_hbm, table_hbm, out_ref, node, table, stage, sems):
    copies = [
        pltpu.make_async_copy(node_hbm, node, sems.at[0]),
        pltpu.make_async_copy(table_hbm, table, sems.at[1]),
    ]
    for copy in copies:
        copy.start()
    copies[1].wait()
    choice = send_choice(table, node.shape[0])
    copies[0].wait()
    stage[...] = dot(choice, node[...]).astype(BF16)
    copy = pltpu.make_async_copy(stage, out_ref, sems.at[0])
    copy.start()
    copy.wait()


def load(sources, targets, sems):
    copies = [
        pltpu.make_async_copy(source, target, sems.at[k])
        for k, (source, target) in enumerate(zip(sources, targets))
    ]
    for copy in copies:
        copy.start()
    return copies


def prepare_kernel(
    live_ref,
    peer_hbm,
    slot_hbm,
    recv_hbm,
    node_hbm,
    first_hbm,
    edge_hbm,
    node_first_hbm,
    second_hbm,
    part_ref,
    far_ref,
    top_ref,
    second_ref,
    node_part_ref,
    receive_ref,
    place_ref,
    peer_ref,
    slot_ref,
    recv_ref,
    node,
    first,
    edge,
    node_first,
    node_part,
    receive,
    places,
    table,
    sems,
    out_sems,
):
    nodes, width = node.shape
    copies = load(
        (
            peer_hbm,
            slot_hbm,
            recv_hbm,
            node_hbm,
            first_hbm,
            edge_hbm,
            node_first_hbm.at[pl.ds(0, width)],
            second_hbm,
            first_hbm.at[pl.ds(0, width)],
        ),
        (peer_ref, slot_ref, recv_ref, node, first, edge, node_first, second_ref, top_ref),
        sems,
    )
    own = lax.axis_index("space")
    blocks = peer_ref.shape[0]
    halo_rows = far_ref.shape[1]
    capacity = halo_rows // lax.axis_size("space")
    for k in range(3):
        copies[k].wait()
    near = []
    for b in range(blocks):
        rows = pl.ds(b * EDGE_BLOCK, EDGE_BLOCK)
        peer, slot, recv = (ref[b : b + 1, :] for ref in (peer_ref, slot_ref, recv_ref))
        mine = peer == own
        far = peer * capacity + slot
        near.append(chosen(jnp.where(mine, slot, -1), nodes))
        far_ref[rows, :] = chosen(jnp.where(mine, -1, far), halo_rows)
        received = jnp.where(b < live_ref[0], recv, -1)
        receive[rows, :] = chosen(received, nodes)
        places[0 : nodes + halo_rows, rows] = chosen_transposed(
            jnp.where(mine, slot, nodes + far), nodes + halo_rows
        )
        places[nodes + halo_rows :, rows] = chosen_transposed(received, nodes)
    out_copies = load((receive, places), (receive_ref, place_ref), out_sems)
    copies[3].wait()
    copies[4].wait()
    table[0:nodes] = dot(node[...], first[0:width]).astype(BF16)
    table[nodes:] = dot(node[...], first[width : 2 * width]).astype(BF16)
    copies[5].wait()
    count = CHUNK // EDGE_BLOCK
    for c in range(blocks // count):
        rows = pl.ds(c * CHUNK, CHUNK)
        choice = jnp.concatenate(
            [jnp.concatenate(near[c * count : (c + 1) * count], axis=0), receive[rows, :]], axis=1
        )
        part_ref[rows, :] = dot(edge[rows, :], first[2 * width :]) + dot(choice, table[...])
    copies[6].wait()
    node_part[...] = dot(node[...], node_first[...])
    out_copies.append(pltpu.make_async_copy(node_part, node_part_ref, out_sems.at[2]))
    out_copies[2].start()
    for copy in (*copies[7:], *out_copies):
        copy.wait()


def forward_kernel(
    part_ref,
    halo_ref,
    far_ref,
    top_ref,
    second_ref,
    gains_hbm,
    place_hbm,
    node_part_hbm,
    node_first_hbm,
    node_second_hbm,
    grad_nodes_hbm,
    slope_ref,
    hidden_ref,
    normed_ref,
    inv_ref,
    grad_agg_ref,
    node_gain_ref,
    aggregate_ref,
    node_hidden_ref,
    node_grad_pre_ref,
    node_grad_post_ref,
    gains,
    place,
    node_part,
    node_first,
    node_second,
    grad_nodes,
    messages,
    sems,
):
    nodes, width = node_part.shape
    copies = load(
        (
            gains_hbm,
            place_hbm.at[pl.ds(place_hbm.shape[0] - nodes, nodes)],
            node_part_hbm,
            node_first_hbm.at[pl.ds(width, width)],
            node_second_hbm,
            grad_nodes_hbm,
        ),
        (gains, place, node_part, node_first, node_second, grad_nodes),
        sems,
    )
    halo_part = dot(halo_ref[...], top_ref[...]).astype(BF16)
    for c in range(part_ref.shape[0] // CHUNK):
        rows = pl.ds(c * CHUNK, CHUNK)
        hidden, slope = activation(part_ref[rows, :] + dot(far_ref[rows, :], halo_part))
        hidden_ref[rows, :] = hidden
        slope_ref[rows, :] = slope.astype(BF16)
        normed, inv_std = normalize(dot(hidden, second_ref[...]))
        normed_ref[rows, :] = normed.astype(BF16)
        inv_ref[rows, :] = jnp.broadcast_to(inv_std, (CHUNK, inv_ref.shape[1]))
        if c == 0:
            copies[0].wait()
        messages[rows, :] = (normed * gains[0:1]).astype(BF16)
    for copy in copies[1:]:
        copy.wait()
    aggregate = dot(place[...], messages[...]).astype(BF16)
    node_hidden, node_slope = activation(node_part[...] + dot(aggregate, node_first[...]))
    node_normed, node_inv = normalize(dot(node_hidden, node_second[...]))
    grad_out = grad_nodes[...].astype(F32)
    node_gain_ref[...] = jnp.sum(grad_out * node_normed, axis=0, keepdims=True)
    grad_post = grad_normalize(grad_out, gains[1:2], node_normed, node_inv)
    grad_pre = (times_transposed(grad_post, node_second[...]) * node_slope).astype(BF16)
    grad_agg_ref[...] = times_transposed(grad_pre, node_first[...]).astype(BF16)
    aggregate_ref[...] = aggregate
    node_hidden_ref[...] = node_hidden
    node_grad_pre_ref[...] = grad_pre
    node_grad_post_ref[...] = grad_post


def backward_kernel(
    live_ref,
    grad_edges_ref,
    slope_ref,
    hidden_ref,
    normed_ref,
    inv_ref,
    grad_agg_ref,
    node_gain_ref,
    aggregate_ref,
    node_hidden_ref,
    node_grad_pre_ref,
    node_grad_post_ref,
    halo_ref,
    second_ref,
    receive_ref,
    gains_ref,
    place_hbm,
    edge_hbm,
    node_hbm,
    grad_post_ref,
    grad_pre_ref,
    placed_ref,
    keep_ref,
    send_ref,
    place,
    edge,
    node,
    node_first,
    node_second,
    edge_first,
    edge_second,
    stage,
    sems,
    load_sems,
):
    width = node.shape[1]
    half = placed_ref.shape[1]
    loads = load((place_hbm, edge_hbm, node_hbm), (place, edge, node), load_sems)
    count = CHUNK // EDGE_BLOCK
    grad_gain = jnp.zeros((1, width), F32)
    for c in range(edge.shape[0] // CHUNK):
        rows = pl.ds(c * CHUNK, CHUNK)
        live = jnp.concatenate(
            [
                jnp.where(jnp.full((EDGE_BLOCK, 1), c * count + k, INT) < live_ref[0], 1.0, 0.0)
                for k in range(count)
            ],
            axis=0,
        )
        grad_out = grad_edges_ref[rows, :].astype(F32) * live + dot(receive_ref[rows, :], grad_agg_ref[...])
        normed = normed_ref[rows, :].astype(F32)
        grad_gain += jnp.sum(grad_out * normed, axis=0, keepdims=True)
        grad_post = grad_normalize(grad_out, gains_ref[0:1], normed, inv_ref[rows, 0:1])
        grad_post_ref[rows, :] = grad_post
        grad_hidden = times_transposed(grad_post, second_ref[...])
        grad_pre_ref[rows, :] = (grad_hidden * slope_ref[rows, :].astype(F32)).astype(BF16)
    for copy in loads:
        copy.wait()
    node_gain = node_gain_ref[...]
    tail = [row[:, half * k : half * (k + 1)] for row in (grad_gain, node_gain) for k in range(2)]
    copies = weight_grads(
        slice(0, half),
        (place, edge, node, halo_ref, hidden_ref, aggregate_ref, node_hidden_ref),
        (grad_pre_ref, grad_post_ref, node_grad_pre_ref, node_grad_post_ref),
        (placed_ref, keep_ref, send_ref, stage, sems),
        (node_first, node_second, edge_first, edge_second),
        [*tail, jnp.zeros((GAIN_ROWS - 4, half), F32)],
    )
    for copy in copies:
        copy.wait()


def right_kernel(
    grad_post_ref,
    grad_pre_ref,
    hidden_ref,
    aggregate_ref,
    node_hidden_ref,
    node_grad_pre_ref,
    node_grad_post_ref,
    halo_ref,
    place_ref,
    edge_ref,
    node_ref,
    placed_ref,
    keep_ref,
    send_ref,
    node_first,
    node_second,
    edge_first,
    edge_second,
    stage,
    sems,
):
    half = placed_ref.shape[1]
    copies = weight_grads(
        slice(half, 2 * half),
        (place_ref, edge_ref, node_ref, halo_ref, hidden_ref, aggregate_ref, node_hidden_ref),
        (grad_pre_ref, grad_post_ref, node_grad_pre_ref, node_grad_post_ref),
        (placed_ref, keep_ref, send_ref, stage, sems),
        (node_first, node_second, edge_first, edge_second),
    )
    for copy in copies:
        copy.wait()


def finish_kernel(
    left_ref,
    right_ref,
    grad_pre_ref,
    node_grad_pre_ref,
    first_hbm,
    node_first_hbm,
    grad_nodes_hbm,
    grad_edges_hbm,
    back_ref,
    edge_out_ref,
    node_total_ref,
    first,
    node_first,
    grad_nodes,
    grad_edges,
    back_stage,
    edge_out,
    node_total,
    sems,
    out_sems,
    edge_sems,
):
    nodes, width = grad_nodes.shape
    loads = load(
        (first_hbm, node_first_hbm.at[pl.ds(0, width)], grad_nodes_hbm, grad_edges_hbm),
        (first, node_first, grad_nodes, grad_edges),
        sems,
    )
    devices, capacity = back_ref.shape[:2]
    far_end = left_ref.shape[0] - nodes
    placed = jnp.concatenate([left_ref[...], right_ref[...]], axis=1)
    loads[0].wait()
    back = times_transposed(placed[nodes:far_end], first[0:width])
    for k in range(devices):
        back_stage[k] = back[k * capacity : (k + 1) * capacity].astype(BF16)
    copies = load((back_stage,), (back_ref,), out_sems)
    loads[1].wait()
    loads[2].wait()
    node_total[...] = (
        grad_nodes[...].astype(F32)
        + times_transposed(node_grad_pre_ref[...], node_first[...])
        + times_transposed(placed[0:nodes], first[0:width])
        + times_transposed(placed[far_end:], first[width : 2 * width])
    )
    copies.append(pltpu.make_async_copy(node_total, node_total_ref, out_sems.at[1]))
    copies[-1].start()
    loads[3].wait()
    for c in range(grad_edges.shape[0] // CHUNK):
        rows = pl.ds(c * CHUNK, CHUNK)
        grad_edge = grad_edges[rows, :].astype(F32) + times_transposed(grad_pre_ref[rows, :], first[2 * width :])
        edge_out[rows, :] = grad_edge.astype(BF16)
        copies.append(pltpu.make_async_copy(edge_out.at[rows], edge_out_ref.at[rows], edge_sems.at[c]))
        copies[-1].start()
    for copy in copies:
        copy.wait()


def nodes_kernel(total_hbm, returned_ref, table_hbm, out_ref, total, table, stage, sems):
    loads = load((total_hbm, table_hbm), (total, table), sems)
    capacity, devices = table.shape[1:]
    returned = jnp.concatenate([returned_ref[k].astype(F32) for k in range(devices)], axis=0).astype(BF16)
    for copy in loads:
        copy.wait()
    choice = send_choice(table, total.shape[0])
    stage[...] = (total[...] + transposed_times(choice, returned)).astype(BF16)
    copy = pltpu.make_async_copy(stage, out_ref, sems.at[0])
    copy.start()
    copy.wait()


def exchange_orders(chips):
    bits = list(range(chips.bit_length() - 1))
    if len(bits) < 3:
        return (bits, bits[::-1]), (bits, bits[::-1])
    first, second, third, *rest = bits
    return (
        ([first, second, third, *rest], [second, first, third, *rest]),
        ([first, third, second, *rest], [third, first, second, *rest]),
    )


def exchange(piece, bits, devices):
    return lax.ppermute(piece, "space", [(i, i ^ (2 << bits[i % 2])) for i in range(devices)])


def half_of(step, bits, positions, away):
    own = lax.axis_index("space")
    core = lax.rem(own, 2)
    bit, position = (pair[0] + core * (pair[1] - pair[0]) for pair in (bits, positions))
    value = lax.shift_right_logical(own, bit + 1) & 1
    value = 1 - value if away else value
    above = lax.shift_right_logical(jnp.int32(step), position)
    low = step - lax.shift_left(above, position)
    return lax.shift_left(above, position + 1) + lax.shift_left(value, position) + low


def fold_kernel(bits, positions, kept_ref, received_ref, *refs):
    sent, kept, stage, sems = refs[-4:]
    copies = []
    for away in (True, False):
        for k in range(kept.shape[0]):
            place = half_of(k, bits, positions, away)
            block = (kept_ref[place].astype(F32) + received_ref[place].astype(F32)).astype(BF16)
            if away:
                stage[k] = block
                copies.append(pltpu.make_async_copy(stage.at[k], sent.at[k], sems.at[k]))
                copies[-1].start()
            else:
                kept[k] = block
    for copy in copies:
        copy.wait()


def shares_kernel(left, left_in, right, right_in, *refs):
    outs, stages, sems = refs[:5], refs[5:10], refs[10]
    sides = [a[0].astype(F32) + b[0].astype(F32) for a, b in ((left, left_in), (right, right_in))]
    rows = sides[1].shape[0]
    total = jnp.concatenate([sides[0][0:rows], sides[1]], axis=1)
    start = 0
    for out, stage in zip(outs[:4], stages):
        stage[...] = total[start : start + out.shape[0]]
        start += out.shape[0]
    gains = [sides[0][rows + k : rows + k + 1] for k in range(4)]
    stages[4][...] = jnp.concatenate(
        [jnp.concatenate(gains[0:2], axis=1), jnp.concatenate(gains[2:4], axis=1)], axis=0
    )
    for copy in load(stages, outs, sems):
        copy.wait()


VMEM, HBM, SMEM = pltpu.VMEM, pltpu.HBM, pltpu.SMEM


def call(body, name, operands, outs, scratch=(), flops=0):
    spaces = [space for _, space in operands]
    arrays = [
        array if space is SMEM else pltpu.with_memory_space_constraint(array, space) for array, space in operands
    ]
    moved = sum(a.size * a.dtype.itemsize for a, _ in operands)
    return pl.pallas_call(
        body,
        in_specs=[pl.BlockSpec(memory_space=space) for space in spaces],
        out_specs=[pl.BlockSpec(memory_space=space) for space, _, _ in outs],
        out_shape=[space(shape, dtype) for space, shape, dtype in outs],
        scratch_shapes=scratch,
        name=name,
        cost_estimate=pl.CostEstimate(flops=flops, bytes_accessed=moved, transcendentals=0),
        compiler_params=pltpu.CompilerParams(vmem_limit_bytes=24 * MIB),
    )(*arrays)


def semaphores(count):
    return pltpu.SemaphoreType.DMA((count,))


def fold_call(name, bits, positions, kept, received, *before):
    shape = (kept.shape[0] // 2, *kept.shape[1:])
    return call(
        functools.partial(fold_kernel, bits, positions),
        name,
        [(kept, VMEM), (received, VMEM), *((a, HBM) for a in before)],
        [(HBM, shape, BF16), (VMEM, shape, BF16)],
        [VMEM(shape, BF16), semaphores(shape[0])],
    )


def shards(
    node_feat,
    edge_feat,
    grad_nodes,
    grad_edges,
    edge_first,
    edge_second,
    node_first,
    node_second,
    gains,
    edge_peer,
    edge_slot,
    edge_recv,
    send_index,
    live_blocks,
):
    nodes, width = node_feat.shape
    edges = edge_feat.shape[0]
    devices, capacity = send_index.shape[1:]
    chips = devices // 2
    halo_rows = devices * capacity
    peer, slot, recv = (a.reshape(edges // EDGE_BLOCK, EDGE_BLOCK) for a in (edge_peer, edge_slot, edge_recv))
    other_core = [(i, i ^ 1) for i in range(devices)]
    block = width * width * 2

    send_table = jnp.swapaxes(send_index, 1, 2)
    (outgoing,) = call(
        outgoing_kernel,
        "outgoing",
        [(node_feat, HBM), (send_table, HBM)],
        [(HBM, (halo_rows, width), BF16)],
        [
            VMEM(node_feat.shape, BF16),
            VMEM(send_table.shape, INT),
            VMEM((halo_rows, width), BF16),
            semaphores(2),
        ],
    )
    halo = lax.all_to_all(
        outgoing.reshape(devices, capacity, width), "space", split_axis=0, concat_axis=0, tiled=True
    ).reshape(halo_rows, width)

    rows_bf16, nodes_f32 = (edges, width), (nodes, width)
    top_shape, place_shape = (width, width), (2 * nodes + halo_rows, edges)
    part, far, top, second, node_part, receive, place = call(
        prepare_kernel,
        "prepare",
        [
            (live_blocks, SMEM),
            *(
                (a, HBM)
                for a in (peer, slot, recv, node_feat, edge_first, edge_feat, node_first, edge_second)
            ),
        ],
        [
            (VMEM, rows_bf16, F32),
            (VMEM, (edges, halo_rows), BF16),
            (VMEM, top_shape, BF16),
            (VMEM, edge_second.shape, BF16),
            (HBM, nodes_f32, F32),
            (HBM, (edges, nodes), BF16),
            (HBM, place_shape, BF16),
        ],
        [
            VMEM(peer.shape, INT),
            VMEM(slot.shape, INT),
            VMEM(recv.shape, INT),
            VMEM(node_feat.shape, BF16),
            VMEM(edge_first.shape, BF16),
            VMEM(edge_feat.shape, BF16),
            VMEM(top_shape, BF16),
            VMEM(nodes_f32, F32),
            VMEM((edges, nodes), BF16),
            VMEM(place_shape, BF16),
            VMEM((2 * nodes, width), BF16),
            semaphores(9),
            semaphores(3),
        ],
        flops=block * (2 * edges + 3 * nodes),
    )

    nodes_bf16 = (VMEM, nodes_f32, BF16)
    kept_rows = (VMEM, rows_bf16, BF16)
    (
        slope,
        hidden,
        normed,
        inv_std,
        grad_agg,
        node_gain,
        aggregate,
        node_hidden,
        node_grad_pre,
        node_grad_post,
    ) = call(
        forward_kernel,
        "forward",
        [
            *((a, VMEM) for a in (part, halo, far, top, second)),
            *((a, HBM) for a in (gains, place, node_part, node_first, node_second, grad_nodes)),
        ],
        [
            kept_rows,
            kept_rows,
            kept_rows,
            (VMEM, (edges, 128), F32),
            nodes_bf16,
            (VMEM, (1, width), F32),
            nodes_bf16,
            nodes_bf16,
            nodes_bf16,
            nodes_bf16,
        ],
        [
            VMEM(gains.shape, F32),
            VMEM((nodes, edges), BF16),
            VMEM(nodes_f32, F32),
            VMEM(top_shape, BF16),
            VMEM(node_second.shape, BF16),
            VMEM(nodes_f32, BF16),
            VMEM(rows_bf16, BF16),
            semaphores(6),
        ],
        flops=block * (2 * edges + 6 * nodes),
    )

    half = width // 2
    weights = (node_first, node_second, edge_first, edge_second)
    share = sum(w.shape[0] // devices for w in weights)
    left_shape, right_shape = (chips, share + GAIN_ROWS, half), (chips, share, half)
    placed = (VMEM, (2 * nodes + halo_rows, half), BF16)
    halves = [VMEM((w.shape[0], half), F32) for w in weights]
    grad_post, grad_pre, left_placed, left_keep, left_send = call(
        backward_kernel,
        "backward",
        [
            (live_blocks, SMEM),
            *(
                (a, VMEM)
                for a in (
                    grad_edges,
                    slope,
                    hidden,
                    normed,
                    inv_std,
                    grad_agg,
                    node_gain,
                    aggregate,
                    node_hidden,
                    node_grad_pre,
                    node_grad_post,
                    halo,
                    second,
                    receive,
                    gains,
                )
            ),
            *((a, HBM) for a in (place, edge_feat, node_feat)),
        ],
        [kept_rows, kept_rows, placed, (VMEM, left_shape, BF16), (HBM, left_shape, BF16)],
        [
            VMEM(place_shape, BF16),
            VMEM(rows_bf16, BF16),
            VMEM(nodes_f32, BF16),
            *halves,
            VMEM(left_shape, BF16),
            semaphores(chips),
            semaphores(3),
        ],
        flops=block * (4 * edges),
    )
    left_received = lax.ppermute(left_send, "space", other_core)
    right_placed, right_keep, right_send = call(
        right_kernel,
        "right",
        [
            (a, VMEM)
            for a in (
                grad_post,
                grad_pre,
                hidden,
                aggregate,
                node_hidden,
                node_grad_pre,
                node_grad_post,
                halo,
                place,
                edge_feat,
                node_feat,
            )
        ],
        [placed, (VMEM, right_shape, BF16), (HBM, right_shape, BF16)],
        [*halves, VMEM(right_shape, BF16), semaphores(chips)],
        flops=block * (2 * edges),
    )
    right_received = lax.ppermute(right_send, "space", other_core)
    back, grad_edge_feat, node_total = call(
        finish_kernel,
        "finish",
        [
            *((a, VMEM) for a in (left_placed, right_placed, grad_pre, node_grad_pre)),
            *((a, HBM) for a in (edge_first, node_first, grad_nodes, grad_edges)),
        ],
        [
            (HBM, (devices, capacity, width), BF16),
            (HBM, rows_bf16, BF16),
            (HBM, nodes_f32, F32),
        ],
        [
            VMEM(edge_first.shape, BF16),
            VMEM(top_shape, BF16),
            VMEM(nodes_f32, BF16),
            VMEM(rows_bf16, BF16),
            VMEM((devices, capacity, width), BF16),
            VMEM(rows_bf16, BF16),
            VMEM(nodes_f32, F32),
            semaphores(4),
            semaphores(2),
            semaphores(edges // CHUNK),
        ],
        flops=block * (edges + 4 * nodes),
    )
    returned = lax.all_to_all(back, "space", split_axis=0, concat_axis=0, tiled=True)

    pieces = [("left", left_keep, left_received), ("right", right_keep, right_received)]
    for stage in range(chips.bit_length() - 1):
        for side, orders in enumerate(exchange_orders(chips)):
            name, kept, received = pieces[side]
            bits = [order[stage] for order in orders]
            positions = [
                order[stage] - sum(earlier < order[stage] for earlier in order[:stage]) for order in orders
            ]
            before = (back,) if stage == 1 and side == 0 else ()
            sent, kept = fold_call(f"{name}_fold", bits, positions, kept, received, *before)
            pieces[side] = (name, kept, exchange(sent, bits, devices))

    (grad_node_feat,) = call(
        nodes_kernel,
        "nodes",
        [(node_total, HBM), (returned, VMEM), (send_table, HBM)],
        [(HBM, nodes_f32, BF16)],
        [VMEM(nodes_f32, F32), VMEM(send_table.shape, INT), VMEM(nodes_f32, BF16), semaphores(2)],
    )
    shapes = [*((w.shape[0] // devices, width) for w in weights), (2, width)]
    grad_node_first, grad_node_second, grad_edge_first, grad_edge_second, gain_totals = call(
        shares_kernel,
        "shares",
        [(a, VMEM) for _, *pair in pieces for a in pair],
        [(HBM, shape, F32) for shape in shapes],
        [*(VMEM(shape, F32) for shape in shapes), semaphores(5)],
    )
    return (
        grad_node_feat,
        grad_edge_feat,
        grad_edge_first,
        grad_edge_second,
        grad_node_first,
        grad_node_second,
        gain_totals,
    )


def solution(mesh):
    placed = (
        P(("group", "space"), None),
        P(("group", "space"), None),
        P(("group", "space"), None),
        P(("group", "space"), None),
        P(),
        P(),
        P(),
        P(),
        P(),
        P(("group", "space")),
        P(("group", "space")),
        P(("group", "space")),
        P(("group", "space"), None, None),
        P(("group", "space")),
    )
    return jax.shard_map(
        shards,
        mesh=mesh,
        in_specs=placed,
        out_specs=(
            P(("group", "space"), None),
            P(("group", "space"), None),
            P(("group", "space"), None),
            P(("group", "space"), None),
            P(("group", "space"), None),
            P(("group", "space"), None),
            P("group", None),
        ),
        check_vma=False,
    )
```

```python
import functools

import jax
import jax.numpy as jnp
from jax import lax
from jax.experimental import pallas as pl
from jax.experimental.pallas import tpu as pltpu
from jax.sharding import PartitionSpec as P

EDGE_BLOCK = 128
CHUNK = 512
GAIN_ROWS = 8
EPS = 1e-05
BF16 = jnp.bfloat16
F32 = jnp.float32
INT = jnp.int32
MIB = 1 << 20


def dot(left, right):
    return lax.dot_general(left, right, (((1,), (0,)), ((), ())), preferred_element_type=F32)


def times_transposed(left, right):
    return lax.dot_general(left, right, (((1,), (1,)), ((), ())), preferred_element_type=F32)


def transposed_times(left, right):
    return lax.dot_general(left, right, (((0,), (0,)), ((), ())), preferred_element_type=F32)


def ones_where(mask):
    return jnp.where(mask, 1.0, 0.0).astype(BF16)


def chosen(row, width):
    lane = lax.broadcasted_iota(INT, (EDGE_BLOCK, EDGE_BLOCK), 1)
    col = jnp.transpose(jnp.broadcast_to(row, (EDGE_BLOCK, EDGE_BLOCK)))
    return jnp.concatenate(
        [ones_where(col == lane + EDGE_BLOCK * j) for j in range(width // EDGE_BLOCK)], axis=1
    )


def chosen_transposed(row, width):
    return ones_where(lax.broadcasted_iota(INT, (width, EDGE_BLOCK), 0) == row)


def send_choice(table_ref, node_rows):
    capacity, devices = table_ref.shape[1:]
    lane = lax.broadcasted_iota(INT, (capacity, node_rows), 1)
    table = table_ref[0]
    out = [jnp.where(table[:, j : j + 1] == lane, 1.0, 0.0) for j in range(devices)]
    return jnp.concatenate(out, axis=0).astype(BF16)


def activation(pre):
    sigmoid = 0.5 * jnp.tanh(0.5 * pre) + 0.5
    hidden = pre * sigmoid
    return hidden.astype(BF16), sigmoid + hidden * (1.0 - sigmoid)


def normalize(post):
    centred = post - jnp.mean(post, axis=-1, keepdims=True)
    inv_std = lax.rsqrt(jnp.mean(centred * centred, axis=-1, keepdims=True) + EPS)
    return centred * inv_std, inv_std


def grad_normalize(grad_out, gain, normed, inv_std):
    grad_normed = grad_out * gain
    return (
        inv_std
        * (
            grad_normed
            - jnp.mean(grad_normed, axis=-1, keepdims=True)
            - normed * jnp.mean(grad_normed * normed, axis=-1, keepdims=True)
        )
    ).astype(BF16)


def pack(keep_ref, send_ref, stage, sems, sources, tail):
    chips = stage.shape[0]
    core = lax.rem(lax.axis_index("space"), 2)
    copies = []
    for away in (True, False):
        for k in range(chips):
            place = 2 * k + 1 - core if away else 2 * k + core
            pieces = []
            for source in sources:
                share = source.shape[0] // (2 * chips)
                pieces.append(source[pl.ds(pl.multiple_of(place * share, 8), share), :])
            rows = jnp.concatenate([*pieces, *tail], axis=0).astype(BF16)
            if away:
                stage[k] = rows
                copies.append(pltpu.make_async_copy(stage.at[k], send_ref.at[k], sems.at[k]))
                copies[-1].start()
            else:
                keep_ref[k] = rows
    return copies


def outgoing_kernel(node_hbm, table_hbm, out_ref, node, table, stage, sems):
    copies = [
        pltpu.make_async_copy(node_hbm, node, sems.at[0]),
        pltpu.make_async_copy(table_hbm, table, sems.at[1]),
    ]
    for copy in copies:
        copy.start()
    copies[1].wait()
    choice = send_choice(table, node.shape[0])
    copies[0].wait()
    stage[...] = dot(choice, node[...]).astype(BF16)
    copy = pltpu.make_async_copy(stage, out_ref, sems.at[0])
    copy.start()
    copy.wait()


def load(sources, targets, sems):
    copies = [
        pltpu.make_async_copy(source, target, sems.at[k])
        for k, (source, target) in enumerate(zip(sources, targets))
    ]
    for copy in copies:
        copy.start()
    return copies


def prepare_kernel(
    live_ref,
    peer_hbm,
    slot_hbm,
    recv_hbm,
    node_hbm,
    first_hbm,
    edge_hbm,
    node_first_hbm,
    second_hbm,
    part_ref,
    far_ref,
    top_ref,
    second_ref,
    node_part_ref,
    receive_ref,
    place_ref,
    peer_ref,
    slot_ref,
    recv_ref,
    node,
    first,
    edge,
    node_first,
    node_part,
    receive,
    places,
    table,
    sems,
    out_sems,
):
    nodes, width = node.shape
    copies = load(
        (
            peer_hbm,
            slot_hbm,
            recv_hbm,
            node_hbm,
            first_hbm,
            edge_hbm,
            node_first_hbm.at[pl.ds(0, width)],
            second_hbm,
            first_hbm.at[pl.ds(0, width)],
        ),
        (peer_ref, slot_ref, recv_ref, node, first, edge, node_first, second_ref, top_ref),
        sems,
    )
    own = lax.axis_index("space")
    blocks = peer_ref.shape[0]
    halo_rows = far_ref.shape[1]
    capacity = halo_rows // lax.axis_size("space")
    for k in range(3):
        copies[k].wait()
    near = []
    for b in range(blocks):
        rows = pl.ds(b * EDGE_BLOCK, EDGE_BLOCK)
        peer, slot, recv = (ref[b : b + 1, :] for ref in (peer_ref, slot_ref, recv_ref))
        mine = peer == own
        far = peer * capacity + slot
        near.append(chosen(jnp.where(mine, slot, -1), nodes))
        far_ref[rows, :] = chosen(jnp.where(mine, -1, far), halo_rows)
        received = jnp.where(b < live_ref[0], recv, -1)
        receive[rows, :] = chosen(received, nodes)
        places[0 : nodes + halo_rows, rows] = chosen_transposed(
            jnp.where(mine, slot, nodes + far), nodes + halo_rows
        )
        places[nodes + halo_rows :, rows] = chosen_transposed(received, nodes)
    out_copies = load((receive, places), (receive_ref, place_ref), out_sems)
    copies[3].wait()
    copies[4].wait()
    table[0:nodes] = dot(node[...], first[0:width]).astype(BF16)
    table[nodes:] = dot(node[...], first[width : 2 * width]).astype(BF16)
    copies[5].wait()
    count = CHUNK // EDGE_BLOCK
    for c in range(blocks // count):
        rows = pl.ds(c * CHUNK, CHUNK)
        choice = jnp.concatenate(
            [jnp.concatenate(near[c * count : (c + 1) * count], axis=0), receive[rows, :]], axis=1
        )
        part_ref[rows, :] = dot(edge[rows, :], first[2 * width :]) + dot(choice, table[...])
    copies[6].wait()
    node_part[...] = dot(node[...], node_first[...])
    out_copies.append(pltpu.make_async_copy(node_part, node_part_ref, out_sems.at[2]))
    out_copies[2].start()
    for copy in (*copies[7:], *out_copies):
        copy.wait()


def forward_kernel(
    part_ref,
    halo_ref,
    far_ref,
    top_ref,
    second_ref,
    gains_hbm,
    place_hbm,
    node_part_hbm,
    node_first_hbm,
    node_second_hbm,
    grad_nodes_hbm,
    slope_ref,
    hidden_ref,
    normed_ref,
    inv_ref,
    grad_agg_ref,
    node_gain_ref,
    aggregate_ref,
    node_hidden_ref,
    node_grad_pre_ref,
    node_grad_post_ref,
    gains,
    place,
    node_part,
    node_first,
    node_second,
    grad_nodes,
    messages,
    sems,
):
    nodes, width = node_part.shape
    copies = load(
        (
            gains_hbm,
            place_hbm.at[pl.ds(place_hbm.shape[0] - nodes, nodes)],
            node_part_hbm,
            node_first_hbm.at[pl.ds(width, width)],
            node_second_hbm,
            grad_nodes_hbm,
        ),
        (gains, place, node_part, node_first, node_second, grad_nodes),
        sems,
    )
    halo_part = dot(halo_ref[...], top_ref[...]).astype(BF16)
    for c in range(part_ref.shape[0] // CHUNK):
        rows = pl.ds(c * CHUNK, CHUNK)
        hidden, slope = activation(part_ref[rows, :] + dot(far_ref[rows, :], halo_part))
        hidden_ref[rows, :] = hidden
        slope_ref[rows, :] = slope.astype(BF16)
        normed, inv_std = normalize(dot(hidden, second_ref[...]))
        normed_ref[rows, :] = normed.astype(BF16)
        inv_ref[rows, :] = jnp.broadcast_to(inv_std, (CHUNK, inv_ref.shape[1]))
        if c == 0:
            copies[0].wait()
        messages[rows, :] = (normed * gains[0:1]).astype(BF16)
    for copy in copies[1:]:
        copy.wait()
    aggregate = dot(place[...], messages[...]).astype(BF16)
    node_hidden, node_slope = activation(node_part[...] + dot(aggregate, node_first[...]))
    node_normed, node_inv = normalize(dot(node_hidden, node_second[...]))
    grad_out = grad_nodes[...].astype(F32)
    node_gain_ref[...] = jnp.sum(grad_out * node_normed, axis=0, keepdims=True)
    grad_post = grad_normalize(grad_out, gains[1:2], node_normed, node_inv)
    grad_pre = (times_transposed(grad_post, node_second[...]) * node_slope).astype(BF16)
    grad_agg_ref[...] = times_transposed(grad_pre, node_first[...]).astype(BF16)
    aggregate_ref[...] = aggregate
    node_hidden_ref[...] = node_hidden
    node_grad_pre_ref[...] = grad_pre
    node_grad_post_ref[...] = grad_post


def backward_kernel(
    live_ref,
    grad_edges_ref,
    hidden_ref,
    normed_ref,
    inv_ref,
    grad_agg_ref,
    node_gain_ref,
    aggregate_ref,
    node_hidden_ref,
    node_grad_pre_ref,
    node_grad_post_ref,
    receive_ref,
    gains_ref,
    node_hbm,
    grad_post_ref,
    keep_ref,
    send_ref,
    node,
    node_first,
    node_second,
    edge_second,
    stage,
    sems,
    load_sem,
):
    width = node.shape[1]
    loads = load((node_hbm,), (node,), load_sem)
    count = CHUNK // EDGE_BLOCK
    grad_gain = jnp.zeros((1, width), F32)
    for c in range(grad_edges_ref.shape[0] // CHUNK):
        rows = pl.ds(c * CHUNK, CHUNK)
        live = jnp.concatenate(
            [
                jnp.where(jnp.full((EDGE_BLOCK, 1), c * count + k, INT) < live_ref[0], 1.0, 0.0)
                for k in range(count)
            ],
            axis=0,
        )
        grad_out = grad_edges_ref[rows, :].astype(F32) * live + dot(receive_ref[rows, :], grad_agg_ref[...])
        normed = normed_ref[rows, :].astype(F32)
        grad_gain += jnp.sum(grad_out * normed, axis=0, keepdims=True)
        grad_post_ref[rows, :] = grad_normalize(grad_out, gains_ref[0:1], normed, inv_ref[rows, 0:1])
    grad_pre = node_grad_pre_ref[...]
    node_second[...] = transposed_times(node_hidden_ref[...], node_grad_post_ref[...])
    node_first[width:] = transposed_times(aggregate_ref[...], grad_pre)
    for copy in loads:
        copy.wait()
    node_first[0:width] = transposed_times(node[...], grad_pre)
    edge_second[...] = transposed_times(hidden_ref[...], grad_post_ref[...])
    tail = (grad_gain, node_gain_ref[...], jnp.zeros((GAIN_ROWS - 2, width), F32))
    for copy in pack(keep_ref, send_ref, stage, sems, (node_first, node_second, edge_second), tail):
        copy.wait()


def right_kernel(
    grad_post_ref,
    slope_ref,
    second_ref,
    halo_ref,
    place_ref,
    edge_ref,
    node_ref,
    grad_pre_ref,
    placed_ref,
    keep_ref,
    send_ref,
    first,
    stage,
    sems,
):
    nodes, width = node_ref.shape
    far_end = place_ref.shape[0] - nodes
    for c in range(edge_ref.shape[0] // CHUNK):
        rows = pl.ds(c * CHUNK, CHUNK)
        grad_hidden = times_transposed(grad_post_ref[rows, :], second_ref[...])
        grad_pre_ref[rows, :] = (grad_hidden * slope_ref[rows, :].astype(F32)).astype(BF16)
    placed = dot(place_ref[...], grad_pre_ref[...]).astype(BF16)
    placed_ref[...] = placed
    first[2 * width :] = transposed_times(edge_ref[...], grad_pre_ref[...])
    first[0:width] = transposed_times(node_ref[...], placed[0:nodes]) + transposed_times(
        halo_ref[...], placed[nodes:far_end]
    )
    first[width : 2 * width] = transposed_times(node_ref[...], placed[far_end:])
    for copy in pack(keep_ref, send_ref, stage, sems, (first,), ()):
        copy.wait()


def finish_kernel(
    placed_ref,
    grad_pre_ref,
    node_grad_pre_ref,
    first_hbm,
    node_first_hbm,
    grad_nodes_hbm,
    grad_edges_hbm,
    back_ref,
    edge_out_ref,
    node_total_ref,
    first,
    node_first,
    grad_nodes,
    grad_edges,
    back_stage,
    edge_out,
    node_total,
    sems,
    out_sems,
    edge_sems,
):
    nodes, width = grad_nodes.shape
    loads = load(
        (first_hbm, node_first_hbm.at[pl.ds(0, width)], grad_nodes_hbm, grad_edges_hbm),
        (first, node_first, grad_nodes, grad_edges),
        sems,
    )
    devices, capacity = back_ref.shape[:2]
    far_end = placed_ref.shape[0] - nodes
    placed = placed_ref[...]
    loads[0].wait()
    back = times_transposed(placed[nodes:far_end], first[0:width])
    for k in range(devices):
        back_stage[k] = back[k * capacity : (k + 1) * capacity].astype(BF16)
    copies = load((back_stage,), (back_ref,), out_sems)
    loads[1].wait()
    loads[2].wait()
    node_total[...] = (
        grad_nodes[...].astype(F32)
        + times_transposed(node_grad_pre_ref[...], node_first[...])
        + times_transposed(placed[0:nodes], first[0:width])
        + times_transposed(placed[far_end:], first[width : 2 * width])
    )
    copies.append(pltpu.make_async_copy(node_total, node_total_ref, out_sems.at[1]))
    copies[-1].start()
    loads[3].wait()
    for c in range(grad_edges.shape[0] // CHUNK):
        rows = pl.ds(c * CHUNK, CHUNK)
        grad_edge = grad_edges[rows, :].astype(F32) + times_transposed(grad_pre_ref[rows, :], first[2 * width :])
        edge_out[rows, :] = grad_edge.astype(BF16)
        copies.append(pltpu.make_async_copy(edge_out.at[rows], edge_out_ref.at[rows], edge_sems.at[c]))
        copies[-1].start()
    for copy in copies:
        copy.wait()


def nodes_kernel(total_hbm, returned_ref, table_hbm, out_ref, total, table, stage, sems):
    loads = load((total_hbm, table_hbm), (total, table), sems)
    capacity, devices = table.shape[1:]
    returned = jnp.concatenate([returned_ref[k].astype(F32) for k in range(devices)], axis=0).astype(BF16)
    for copy in loads:
        copy.wait()
    choice = send_choice(table, total.shape[0])
    stage[...] = (total[...] + transposed_times(choice, returned)).astype(BF16)
    copy = pltpu.make_async_copy(stage, out_ref, sems.at[0])
    copy.start()
    copy.wait()


def exchange_orders(chips):
    bits = list(range(chips.bit_length() - 1))
    if len(bits) < 3:
        return (bits, bits[::-1]), (bits, bits[::-1])
    first, second, third, *rest = bits
    return (
        ([first, second, third, *rest], [second, third, first, *rest]),
        ([first, second, third, *rest], [third, first, second, *rest]),
    )


def exchange(piece, bits, devices):
    return lax.ppermute(piece, "space", [(i, i ^ (2 << bits[i % 2])) for i in range(devices)])


def half_of(step, bits, positions, away):
    own = lax.axis_index("space")
    core = lax.rem(own, 2)
    bit, position = (pair[0] + core * (pair[1] - pair[0]) for pair in (bits, positions))
    value = lax.shift_right_logical(own, bit + 1) & 1
    value = 1 - value if away else value
    above = lax.shift_right_logical(jnp.int32(step), position)
    low = step - lax.shift_left(above, position)
    return lax.shift_left(above, position + 1) + lax.shift_left(value, position) + low


def fold_kernel(bits, positions, kept_ref, received_ref, *refs):
    sent, kept, stage, sems = refs[-4:]
    copies = []
    for away in (True, False):
        for k in range(kept.shape[0]):
            place = half_of(k, bits, positions, away)
            block = (kept_ref[place].astype(F32) + received_ref[place].astype(F32)).astype(BF16)
            if away:
                stage[k] = block
                copies.append(pltpu.make_async_copy(stage.at[k], sent.at[k], sems.at[k]))
                copies[-1].start()
            else:
                kept[k] = block
    for copy in copies:
        copy.wait()


def shares_kernel(count, kept, received, *refs):
    outs, stages, sems = refs[-2 * count - 1 : -count - 1], refs[-count - 1 : -1], refs[-1]
    total = kept[0].astype(F32) + received[0].astype(F32)
    start = 0
    for stage in stages:
        stage[...] = total[start : start + stage.shape[0]]
        start += stage.shape[0]
    for copy in load(stages, outs, sems):
        copy.wait()


VMEM, HBM, SMEM = pltpu.VMEM, pltpu.HBM, pltpu.SMEM


def call(body, name, operands, outs, scratch=(), flops=0):
    spaces = [space for _, space in operands]
    arrays = [
        array if space is SMEM else pltpu.with_memory_space_constraint(array, space) for array, space in operands
    ]
    moved = sum(a.size * a.dtype.itemsize for a, _ in operands)
    return pl.pallas_call(
        body,
        in_specs=[pl.BlockSpec(memory_space=space) for space in spaces],
        out_specs=[pl.BlockSpec(memory_space=space) for space, _, _ in outs],
        out_shape=[space(shape, dtype) for space, shape, dtype in outs],
        scratch_shapes=scratch,
        name=name,
        cost_estimate=pl.CostEstimate(flops=flops, bytes_accessed=moved, transcendentals=0),
        compiler_params=pltpu.CompilerParams(vmem_limit_bytes=24 * MIB),
    )(*arrays)


def semaphores(count):
    return pltpu.SemaphoreType.DMA((count,))


def fold_call(name, bits, positions, kept, received, *before):
    shape = (kept.shape[0] // 2, *kept.shape[1:])
    return call(
        functools.partial(fold_kernel, bits, positions),
        name,
        [(kept, VMEM), (received, VMEM), *((a, HBM) for a in before)],
        [(HBM, shape, BF16), (VMEM, shape, BF16)],
        [VMEM(shape, BF16), semaphores(shape[0])],
    )


def share_call(name, kept, received, shapes, *before):
    return call(
        functools.partial(shares_kernel, len(shapes)),
        f"{name}_shares",
        [(kept, VMEM), (received, VMEM), *((a, HBM) for a in before)],
        [(HBM, shape, F32) for shape in shapes],
        [*(VMEM(shape, F32) for shape in shapes), semaphores(len(shapes))],
    )


def shards(
    node_feat,
    edge_feat,
    grad_nodes,
    grad_edges,
    edge_first,
    edge_second,
    node_first,
    node_second,
    gains,
    edge_peer,
    edge_slot,
    edge_recv,
    send_index,
    live_blocks,
):
    nodes, width = node_feat.shape
    edges = edge_feat.shape[0]
    devices, capacity = send_index.shape[1:]
    chips = devices // 2
    halo_rows = devices * capacity
    peer, slot, recv = (a.reshape(edges // EDGE_BLOCK, EDGE_BLOCK) for a in (edge_peer, edge_slot, edge_recv))
    other_core = [(i, i ^ 1) for i in range(devices)]
    block = width * width * 2

    send_table = jnp.swapaxes(send_index, 1, 2)
    (outgoing,) = call(
        outgoing_kernel,
        "outgoing",
        [(node_feat, HBM), (send_table, HBM)],
        [(HBM, (halo_rows, width), BF16)],
        [
            VMEM(node_feat.shape, BF16),
            VMEM(send_table.shape, INT),
            VMEM((halo_rows, width), BF16),
            semaphores(2),
        ],
    )
    halo = lax.all_to_all(
        outgoing.reshape(devices, capacity, width), "space", split_axis=0, concat_axis=0, tiled=True
    ).reshape(halo_rows, width)

    rows_bf16, nodes_f32 = (edges, width), (nodes, width)
    top_shape, place_shape = (width, width), (2 * nodes + halo_rows, edges)
    part, far, top, second, node_part, receive, place = call(
        prepare_kernel,
        "prepare",
        [
            (live_blocks, SMEM),
            *(
                (a, HBM)
                for a in (peer, slot, recv, node_feat, edge_first, edge_feat, node_first, edge_second)
            ),
        ],
        [
            (VMEM, rows_bf16, F32),
            (VMEM, (edges, halo_rows), BF16),
            (VMEM, top_shape, BF16),
            (VMEM, edge_second.shape, BF16),
            (HBM, nodes_f32, F32),
            (HBM, (edges, nodes), BF16),
            (HBM, place_shape, BF16),
        ],
        [
            VMEM(peer.shape, INT),
            VMEM(slot.shape, INT),
            VMEM(recv.shape, INT),
            VMEM(node_feat.shape, BF16),
            VMEM(edge_first.shape, BF16),
            VMEM(edge_feat.shape, BF16),
            VMEM(top_shape, BF16),
            VMEM(nodes_f32, F32),
            VMEM((edges, nodes), BF16),
            VMEM(place_shape, BF16),
            VMEM((2 * nodes, width), BF16),
            semaphores(9),
            semaphores(3),
        ],
        flops=block * (2 * edges + 3 * nodes),
    )

    nodes_bf16 = (VMEM, nodes_f32, BF16)
    kept_rows = (VMEM, rows_bf16, BF16)
    (
        slope,
        hidden,
        normed,
        inv_std,
        grad_agg,
        node_gain,
        aggregate,
        node_hidden,
        node_grad_pre,
        node_grad_post,
    ) = call(
        forward_kernel,
        "forward",
        [
            *((a, VMEM) for a in (part, halo, far, top, second)),
            *((a, HBM) for a in (gains, place, node_part, node_first, node_second, grad_nodes)),
        ],
        [
            kept_rows,
            kept_rows,
            kept_rows,
            (VMEM, (edges, 128), F32),
            nodes_bf16,
            (VMEM, (1, width), F32),
            nodes_bf16,
            nodes_bf16,
            nodes_bf16,
            nodes_bf16,
        ],
        [
            VMEM(gains.shape, F32),
            VMEM((nodes, edges), BF16),
            VMEM(nodes_f32, F32),
            VMEM(top_shape, BF16),
            VMEM(node_second.shape, BF16),
            VMEM(nodes_f32, BF16),
            VMEM(rows_bf16, BF16),
            semaphores(6),
        ],
        flops=block * (2 * edges + 6 * nodes),
    )

    node_shares = [(w.shape[0] // devices, width) for w in (node_first, node_second)]
    edge_shares = [(w.shape[0] // devices, width) for w in (edge_first, edge_second)]
    left_shares = [*node_shares, edge_shares[1], (2, width)]
    left_shape = (chips, sum(rows for rows, _ in left_shares[:3]) + GAIN_ROWS, width)
    right_shape = (chips, edge_shares[0][0], width)
    placed_shape = (2 * nodes + halo_rows, width)
    grad_post, left_keep, left_send = call(
        backward_kernel,
        "backward",
        [
            (live_blocks, SMEM),
            *(
                (a, VMEM)
                for a in (
                    grad_edges,
                    hidden,
                    normed,
                    inv_std,
                    grad_agg,
                    node_gain,
                    aggregate,
                    node_hidden,
                    node_grad_pre,
                    node_grad_post,
                    receive,
                    gains,
                )
            ),
            (node_feat, HBM),
        ],
        [kept_rows, (VMEM, left_shape, BF16), (HBM, left_shape, BF16)],
        [
            VMEM(nodes_f32, BF16),
            VMEM(node_first.shape, F32),
            VMEM(node_second.shape, F32),
            VMEM(edge_second.shape, F32),
            VMEM(left_shape, BF16),
            semaphores(chips),
            semaphores(1),
        ],
        flops=block * (2 * edges + 3 * nodes),
    )
    left_received = lax.ppermute(left_send, "space", other_core)
    grad_pre, placed, right_keep, right_send = call(
        right_kernel,
        "right",
        [(a, VMEM) for a in (grad_post, slope, second, halo, place, edge_feat, node_feat)],
        [kept_rows, (VMEM, placed_shape, BF16), (VMEM, right_shape, BF16), (HBM, right_shape, BF16)],
        [VMEM(edge_first.shape, F32), VMEM(right_shape, BF16), semaphores(chips)],
        flops=block * (4 * edges),
    )
    right_received = lax.ppermute(right_send, "space", other_core)
    back, grad_edge_feat, node_total = call(
        finish_kernel,
        "finish",
        [
            *((a, VMEM) for a in (placed, grad_pre, node_grad_pre)),
            *((a, HBM) for a in (edge_first, node_first, grad_nodes, grad_edges)),
        ],
        [
            (HBM, (devices, capacity, width), BF16),
            (HBM, rows_bf16, BF16),
            (HBM, nodes_f32, F32),
        ],
        [
            VMEM(edge_first.shape, BF16),
            VMEM(top_shape, BF16),
            VMEM(nodes_f32, BF16),
            VMEM(rows_bf16, BF16),
            VMEM((devices, capacity, width), BF16),
            VMEM(rows_bf16, BF16),
            VMEM(nodes_f32, F32),
            semaphores(4),
            semaphores(2),
            semaphores(edges // CHUNK),
        ],
        flops=block * (edges + 4 * nodes),
    )
    returned = lax.all_to_all(back, "space", split_axis=0, concat_axis=0, tiled=True)

    pieces = [("left", left_keep, left_received), ("right", right_keep, right_received)]
    for stage in range(chips.bit_length() - 1):
        for side, orders in enumerate(exchange_orders(chips)):
            name, kept, received = pieces[side]
            bits = [order[stage] for order in orders]
            positions = [
                order[stage] - sum(earlier < order[stage] for earlier in order[:stage]) for order in orders
            ]
            before = (back,) if stage == 1 and side == 0 else ()
            sent, kept = fold_call(f"{name}_fold", bits, positions, kept, received, *before)
            pieces[side] = (name, kept, exchange(sent, bits, devices))

    (grad_node_feat,) = call(
        nodes_kernel,
        "nodes",
        [(node_total, HBM), (returned, VMEM), (send_table, HBM)],
        [(HBM, nodes_f32, BF16)],
        [VMEM(nodes_f32, F32), VMEM(send_table.shape, INT), VMEM(nodes_f32, BF16), semaphores(2)],
    )
    grad_node_first, grad_node_second, grad_edge_second, gain_totals = share_call(*pieces[0], left_shares)
    (grad_edge_first,) = share_call(*pieces[1], edge_shares[:1], gain_totals)
    return (
        grad_node_feat,
        grad_edge_feat,
        grad_edge_first,
        grad_edge_second,
        grad_node_first,
        grad_node_second,
        gain_totals,
    )


def solution(mesh):
    placed = (
        P(("group", "space"), None),
        P(("group", "space"), None),
        P(("group", "space"), None),
        P(("group", "space"), None),
        P(),
        P(),
        P(),
        P(),
        P(),
        P(("group", "space")),
        P(("group", "space")),
        P(("group", "space")),
        P(("group", "space"), None, None),
        P(("group", "space")),
    )
    return jax.shard_map(
        shards,
        mesh=mesh,
        in_specs=placed,
        out_specs=(
            P(("group", "space"), None),
            P(("group", "space"), None),
            P(("group", "space"), None),
            P(("group", "space"), None),
            P(("group", "space"), None),
            P(("group", "space"), None),
            P("group", None),
        ),
        check_vma=False,
    )
```
